512 devices in a mesh: blk: 32 (over x, z_hi, core), uly: 16 (over y, z_lo).
Axes of the slice: x: 4, y: 8, z: 8 (z_hi: 4, z_lo: 2; z = z_hi * 2 + z_lo), core: 2. Of those that a mesh axis runs over, the one named last changes fastest.
Arguments:
- queries: bfloat16 [32768, 1536], P(('blk', 'uly')), may hold values from -6 to 6, as said below
- keys: bfloat16 [32768, 1536], P(('blk', 'uly')), may hold values from -6 to 6, as said below
- values: bfloat16 [32768, 1536], P(('blk', 'uly')), may hold values from -6 to 6
- block_mask: int32 [12, 256, 256], P(None, 'blk'), may hold values from 0 to 1, as said below
Outputs:
- attended: bfloat16 [32768, 1536], P(('blk', 'uly'))
The draws below stay inside these ranges and needn't reach their ends.
Inputs may be any that keep to these rules, and one draw needn't show every extreme that they name: `queries`: drawn like normal activations; a few rows may point along a common direction. `keys`: drawn like normal activations; a few rows may point along a common direction. `block_mask`: for every head and query block, each aligned group of 8 key blocks holds exactly one 1; every diagonal block is 1.
All inputs are finite; a program needn't handle non-finite values.
Results may differ from the reference program's by a relative error of at most 0.0095.
Values may be sent and summed in bfloat16 or wider, within the bound.
No kernel may reach another device: no remote copies, remote signals or barrier semaphores. Data moves between devices by JAX's collectives and lax.ppermute only.
A program may use at most 64 MiB of HBM per device.

```python
import jax
import jax.numpy as jnp
from jax import lax

H = 12
HD = 128
BS = 128
SEQ = 32768
NB = 256
SEGB = 8


def draw_queries(key, part):
    key = jax.random.fold_in(key, 11)
    k_one = jax.random.fold_in(key, 0)
    field = jnp.clip(jax.random.normal(k_one, (SEQ, H * HD), jnp.float32), -6.0, 6.0)
    return field.astype(jnp.bfloat16)


def draw_keys(key, part):
    key = jax.random.fold_in(key, 23)
    k_one = jax.random.fold_in(key, 0)
    field = jnp.clip(jax.random.normal(k_one, (SEQ, H * HD), jnp.float32), -6.0, 6.0)
    return field.astype(jnp.bfloat16)


def draw_block_mask(key, part):
    key = jax.random.fold_in(key, 37)
    groups = NB // SEGB
    rolls = jax.random.randint(key, (H, NB, groups), 0, SEGB)
    rows = jnp.arange(NB, dtype=jnp.int32)
    group_ids = jnp.arange(groups, dtype=jnp.int32)
    own_group = rows // SEGB
    own_offset = rows % SEGB
    same = group_ids[None, :] == own_group[:, None]
    rolls = jnp.where(same[None, :, :], jnp.broadcast_to(own_offset[None, :, None], rolls.shape), rolls)
    columns = jnp.arange(NB, dtype=jnp.int32)
    spread_rolls = rolls[:, :, columns // SEGB]
    live = spread_rolls == (columns % SEGB)[None, None, :]
    return live.astype(jnp.int32)


def block_levels(stream_key, extent, cuts, smallest, top_value):
    factor_of, own = 1.0, jax.random.fold_in(stream_key, 6)
    for dim, blocks in cuts:
        steps = jnp.exp(jax.random.uniform(jax.random.fold_in(own, dim), (blocks,), jnp.float32, smallest / len(cuts), top_value / len(cuts)))
        factor_of = factor_of * jnp.repeat(steps, extent[dim] // blocks).reshape([-1 if axis == dim else 1 for axis in range(len(extent))])
    return factor_of


def normal_values(own_key, extent, width, limit, cuts=(), kind=jnp.bfloat16):
    loudness = block_levels(own_key, extent, cuts, -0.22, 0.18) if cuts else 1.0
    array = jax.random.normal(own_key, extent, jnp.float32) * width * loudness
    return jnp.minimum(jnp.maximum(array, -limit), limit).astype(kind)


def setup_inputs(seed: int = 0) -> dict:
    splits = jax.random.split(jax.random.key(seed), 5)
    queries = draw_queries(jax.random.fold_in(splits[4], 71), 0)
    keys = draw_keys(jax.random.fold_in(splits[4], 71), 0)
    values = normal_values(splits[2], (SEQ, H * HD), 1.0, 6.0, ((0, 512),))
    block_mask = draw_block_mask(jax.random.fold_in(splits[4], 71), 0)
    return dict(queries=queries, keys=keys, values=values, block_mask=block_mask)


def one_head(inputs):
    qh, kh, vh, mh = inputs
    scale = 1.0 / jnp.sqrt(jnp.float32(HD))
    qblocks = qh.reshape(NB, BS, HD)
    kblocks = kh.reshape(NB, BS, HD)
    vblocks = vh.reshape(NB, BS, HD)
    offsets = (jnp.arange(NB, dtype=jnp.int32) % SEGB).astype(jnp.int32)
    groups = NB // SEGB
    bases = (jnp.arange(groups, dtype=jnp.int32) * SEGB).astype(jnp.int32)

    def one_block(pair):
        qb, mrow = pair
        picks = lax.optimization_barrier(jnp.sum((mrow * offsets).reshape(groups, SEGB), axis=1)).astype(jnp.int32) + bases
        chosen_k = kblocks[picks].reshape(groups * BS, HD)
        chosen_v = vblocks[picks].reshape(groups * BS, HD)
        scores = jnp.dot(qb, chosen_k.T, preferred_element_type=jnp.float32) * scale
        peak = lax.optimization_barrier(jnp.max(scores, axis=1))
        weights = jnp.exp(scores - peak[:, None])
        total = lax.optimization_barrier(jnp.sum(weights, axis=1))
        out = jnp.dot(weights.astype(jnp.bfloat16), chosen_v, preferred_element_type=jnp.float32)
        return (out / total[:, None]).astype(jnp.bfloat16)
    return lax.map(one_block, (qblocks, mh))

def reference(queries, keys, values, block_mask):
    qs = queries.reshape(SEQ, H, HD).transpose(1, 0, 2)
    ks = keys.reshape(SEQ, H, HD).transpose(1, 0, 2)
    vs = values.reshape(SEQ, H, HD).transpose(1, 0, 2)
    outs = lax.map(one_head, (qs, ks, vs, block_mask))
    return outs.reshape(H, SEQ, HD).transpose(1, 0, 2).reshape(SEQ, H * HD)
```

```python
import functools
import math

import jax
import jax.numpy as jnp
from jax import lax
from jax.experimental import pallas as pl
from jax.experimental.pallas import tpu as pltpu
from jax.sharding import PartitionSpec as P

BF = jnp.bfloat16
F32 = jnp.float32
NX, NZ, NC, NU = 4, 4, 2, 16
HEADS, HD, BS, TOK = 12, 128, 128, 64
SEGB = 8
EXTRA = 16
LSE = 32
VMEM = pl.BlockSpec(memory_space=pltpu.VMEM)
SMEM = pl.BlockSpec(memory_space=pltpu.SMEM)


def blk_perm(dx, dz, dc):
    pairs = []
    for x in range(NX):
        for z in range(NZ):
            for c in range(NC):
                to = ((x + dx) % NX * NZ + (z + dz) % NZ) * NC + (c ^ dc)
                pairs.append(((x * NZ + z) * NC + c, to))
    return pairs


def shift(field, dx, dz, dc):
    return lax.ppermute(field, "blk", blk_perm(dx, dz, dc))


def pack_kernel(head_ref, q_ref, k_ref, v_ref, mask_ref, out_ref, picks_ref):
    for h in range(HEADS):
        lanes = slice(h * HD, (h + 1) * HD)
        out_ref[h, 0:TOK, :] = q_ref[:, lanes]
        out_ref[h, TOK : 2 * TOK, :] = k_ref[:, lanes]
        out_ref[h, 2 * TOK : 3 * TOK, :] = v_ref[:, lanes]
    for s in range(HEADS, NU):
        out_ref[s] = jnp.zeros((3 * TOK, HD), BF)
    live = mask_ref[head_ref[0]].astype(F32).astype(BF)
    rows, cols = live.shape
    i = lax.broadcasted_iota(jnp.int32, (cols, HD), 0)
    g = lax.broadcasted_iota(jnp.int32, (cols, HD), 1)
    weight = jnp.where(i // SEGB == g, i % SEGB, 0).astype(F32).astype(BF)
    picks = jnp.dot(live, weight, preferred_element_type=F32)
    picks_ref[...] = jnp.concatenate([picks, jnp.zeros((EXTRA - rows, HD), F32)], axis=0).astype(BF)


def attend_kernel(columns_ref, picks_ref, *refs):
    q_refs, kv_refs, out_ref = refs[:NZ], refs[NZ : NZ + NX * NC], refs[-1]
    scale = 1.0 / math.sqrt(HD)
    for z in range(NZ):
        q_ref = q_refs[z]

        def one(qb, carry):
            q = q_ref[pl.ds(pl.multiple_of(qb * BS, BS), BS), :]
            keys, values = [], []
            for c, kv_ref in enumerate(kv_refs):
                j = picks_ref[z * SEGB + qb, columns_ref[c]]
                both = kv_ref[pl.ds(2 * j, 2)]
                keys.append(both[:, :TOK, :].reshape(BS, HD))
                values.append(both[:, TOK:, :].reshape(BS, HD))
            k = jnp.concatenate(keys, axis=0)
            v = jnp.concatenate(values, axis=0)
            s = lax.dot_general(q, k, (((1,), (1,)), ((), ())), preferred_element_type=F32)
            peak = jnp.max(s, axis=1, keepdims=True)
            w = jnp.exp((s - peak) * scale)
            total = jnp.sum(w, axis=1, keepdims=True)
            o = jnp.dot(w.astype(BF), v, preferred_element_type=F32) / total
            out_ref[z, pl.ds(pl.multiple_of(qb * BS, BS), BS), :] = o.astype(BF)
            lse = peak * scale + jnp.log(total)
            lse = jnp.transpose(jnp.broadcast_to(lse, (BS, HD)))[0:1, :]
            row = lax.broadcasted_iota(jnp.int32, (SEGB, HD), 0)
            return jnp.where(row == qb, jnp.broadcast_to(lse, (SEGB, HD)), carry)

        lse = lax.fori_loop(0, SEGB, one, jnp.zeros((SEGB, HD), F32))
        hi = lse.astype(BF).astype(F32)
        mid = (lse - hi).astype(BF).astype(F32)
        low = lse - hi - mid
        out_ref[z, SEGB * BS :, :] = jnp.concatenate([hi, mid, low, jnp.zeros_like(hi)], axis=0).astype(BF)


def merge_kernel(a_ref, b_ref, c_ref, d_ref, out_ref):
    refs = (a_ref, b_ref, c_ref, d_ref)
    lses = []
    for r in refs:
        rows = r[SEGB * BS :, :].astype(F32)
        lses.append(rows[0:SEGB] + rows[SEGB : 2 * SEGB] + rows[2 * SEGB : 3 * SEGB])
    top = functools.reduce(jnp.maximum, lses)
    parts = [jnp.exp(s - top) for s in lses]
    total = functools.reduce(jnp.add, parts)
    parts = [p / total for p in parts]
    for qb in range(SEGB):
        acc = jnp.zeros((BS, HD), F32)
        for r, p in zip(refs, parts):
            w = jnp.transpose(jnp.broadcast_to(p[qb : qb + 1, :], (BS, HD)))
            acc = acc + w * r[qb * BS : (qb + 1) * BS, :].astype(F32)
        out_ref[qb * BS : (qb + 1) * BS, :] = acc.astype(BF)


def unpack_kernel(in_ref, out_ref):
    for h in range(HEADS):
        out_ref[:, h * HD : (h + 1) * HD] = in_ref[h]


def call(kernel, outs, specs, *args, flops=0, moved=1 << 20):
    return pl.pallas_call(
        kernel,
        out_shape=outs,
        in_specs=specs,
        out_specs=jax.tree.map(lambda _: VMEM, outs),
        compiler_params=pltpu.CompilerParams(vmem_limit_bytes=48 << 20),
        cost_estimate=pl.CostEstimate(flops=flops, bytes_accessed=moved, transcendentals=0),
    )(*args)


def shards(queries, keys, values, block_mask):
    here_blk = lax.axis_index("blk")
    here_uly = lax.axis_index("uly")
    x, z, c = here_blk // (NZ * NC), here_blk // NC % NZ, here_blk % NC
    head = jnp.minimum(here_uly, HEADS - 1).reshape(1).astype(jnp.int32)
    packed, picks = call(
        pack_kernel,
        (jax.ShapeDtypeStruct((NU, 3 * TOK, HD), BF), jax.ShapeDtypeStruct((EXTRA, HD), BF)),
        [SMEM, VMEM, VMEM, VMEM, VMEM],
        head, queries, keys, values, block_mask,
    )
    got = lax.all_to_all(packed, "uly", split_axis=0, concat_axis=0, tiled=True)
    q_own = jnp.concatenate([got[:, :TOK].reshape(NU * TOK, HD), picks], axis=0)
    kv_own = got[:, TOK:]

    kvs, columns = [], []
    for dx in range(NX):
        near = kv_own if dx == 0 else shift(kv_own, dx, 0, 0)
        for dc in range(NC):
            kvs.append(near if dc == 0 else shift(near, 0, 0, 1))
            columns.append(((x - dx) % NX * NZ + z) * NC + (c ^ dc))
    qs = [q_own if dz == 0 else shift(q_own, 0, dz, 0) for dz in range(NZ)]
    picks_all = jnp.concatenate([q[NU * TOK : NU * TOK + SEGB] for q in qs], axis=0).astype(jnp.int32)
    parts = call(
        attend_kernel,
        jax.ShapeDtypeStruct((NZ, NU * TOK + LSE, HD), BF),
        [SMEM, SMEM] + [VMEM] * (NZ + NX * NC),
        jnp.stack(columns).astype(jnp.int32), picks_all, *qs, *kvs,
        flops=1 << 31, moved=6 << 20,
    )
    backs = [parts[0]] + [shift(parts[dz], 0, -dz, 0) for dz in range(1, NZ)]
    merged = call(merge_kernel, jax.ShapeDtypeStruct((NU * TOK, HD), BF), [VMEM] * NZ, *backs)
    home = lax.all_to_all(merged.reshape(NU, TOK, HD), "uly", split_axis=0, concat_axis=0, tiled=True)
    return call(unpack_kernel, jax.ShapeDtypeStruct((TOK, HEADS * HD), BF), [VMEM], home)


def solution(mesh):
    placed = (
        P(("blk", "uly"), None),
        P(("blk", "uly"), None),
        P(("blk", "uly"), None),
        P(None, "blk", None),
    )
    return jax.shard_map(
        shards, mesh=mesh, in_specs=placed, out_specs=P(("blk", "uly"), None), check_vma=False
    )
```

```python
import functools
import math

import jax
import jax.numpy as jnp
from jax import lax
from jax.experimental import pallas as pl
from jax.experimental.pallas import tpu as pltpu
from jax.sharding import Mesh, PartitionSpec as P

BF = jnp.bfloat16
F32 = jnp.float32
NX, NZ, NC, NU = 4, 4, 2, 16
HEADS, HD, BS, TOK = 12, 128, 128, 64
SEGB = 8
GROUPS = NX * NC
HALF = 4
ROWS = HALF * BS
EXTRA = 16
EXP2 = math.log2(math.e) / math.sqrt(HD)
AXES = ("x", "zh", "core", "y", "zl")
VMEM = pl.BlockSpec(memory_space=pltpu.VMEM)
SMEM = pl.BlockSpec(memory_space=pltpu.SMEM)
ANY = pl.BlockSpec(memory_space=pl.ANY)


def shift(field, axis, by):
    n = lax.axis_size(axis)
    return lax.ppermute(field, axis, [(i, (i + by) % n) for i in range(n)])


def pack_kernel(head_ref, q_hbm, k_hbm, v_hbm, mask_hbm, out_ref, picks_ref, q_ref, k_ref, v_ref, mask_ref, sems):
    pairs = ((mask_hbm.at[head_ref[0]], mask_ref), (q_hbm, q_ref), (k_hbm, k_ref), (v_hbm, v_ref))
    copies = [pltpu.make_async_copy(src, dst, sems.at[i]) for i, (src, dst) in enumerate(pairs)]
    for copy in copies:
        copy.start()
    for s in range(HEADS, NU):
        out_ref[s] = jnp.zeros((3 * TOK, HD), BF)
    copies[0].wait()
    live = mask_ref[...].astype(F32).astype(BF)
    cols = live.shape[1]
    i = lax.broadcasted_iota(jnp.int32, (cols, HD), 0)
    g = lax.broadcasted_iota(jnp.int32, (cols, HD), 1)
    weight = jnp.where(i // SEGB == g, i % SEGB, 0).astype(F32).astype(BF)
    picks = jnp.dot(live, weight, preferred_element_type=F32)
    pad = jnp.zeros((EXTRA - HALF, HD), F32)
    for half in range(2):
        picks_ref[half] = jnp.concatenate([picks[half * HALF : (half + 1) * HALF], pad], axis=0).astype(BF)
    for n, ref in enumerate((q_ref, k_ref, v_ref)):
        copies[n + 1].wait()
        for h in range(HEADS):
            out_ref[h, n * TOK : (n + 1) * TOK, :] = ref[:, h * HD : (h + 1) * HD]


def split3(lse):
    hi = lse.astype(BF).astype(F32)
    mid = (lse - hi).astype(BF).astype(F32)
    return jnp.concatenate([hi, mid, lse - hi - mid, jnp.zeros_like(hi)], axis=0).astype(BF)


def join3(rows):
    rows = rows.astype(F32)
    return rows[0:HALF] + rows[HALF : 2 * HALF] + rows[2 * HALF : 3 * HALF]


def attend_kernel(halves, n_kv, columns_ref, picks_ref, *refs):
    n_q = len(set(ref for ref, _ in halves))
    q_refs, kv_refs, out_refs = refs[:n_q], refs[n_q : n_q + n_kv], refs[n_q + n_kv :]
    groups = kv_refs if n_kv == GROUPS else [kv_refs[0].at[g] for g in range(GROUPS)]
    columns = [columns_ref[g] for g in range(GROUPS)]
    blocks = [(h, b) for h in range(len(halves)) for b in range(HALF)]
    n = len(blocks)
    fetched, scores, weights, peaks, totals = {}, {}, {}, {}, {}
    lses = [[] for _ in halves]
    for t in range(n + 2):
        ahead, here, last = t, t - 1, t - 2
        if ahead < n:
            h, b = blocks[ahead]
            ref, part = halves[h]
            q = (q_refs[ref] if part is None else q_refs[ref].at[part])[b * BS : (b + 1) * BS, :]
            keys, values = [], []
            for g in range(GROUPS):
                j = picks_ref[h * HALF + b, columns[g]]
                both = groups[g][pl.ds(2 * j, 2)]
                keys.append(both[:, :TOK, :].reshape(BS, HD))
                values.append(both[:, TOK:, :].reshape(BS, HD))
            fetched[ahead], scores[ahead] = (q, keys, values), []
        if 0 <= here < n:
            weights[here], peaks[here], totals[here] = [], [], []
        acc = None
        for step in range(4):
            if ahead < n:
                q, keys, _ = fetched[ahead]
                pair = jnp.concatenate(keys[2 * step : 2 * step + 2], axis=0)
                scores[ahead].append(
                    lax.dot_general(q, pair, (((1,), (1,)), ((), ())), preferred_element_type=F32)
                )
            if 0 <= here < n:
                rows = slice(step * BS // 4, (step + 1) * BS // 4)
                part = [s[rows] for s in scores[here]]
                peak = jnp.max(functools.reduce(jnp.maximum, part), axis=1, keepdims=True)
                w = [jnp.exp2((s - peak) * EXP2) for s in part]
                totals[here].append(jnp.sum(functools.reduce(jnp.add, w), axis=1, keepdims=True))
                peaks[here].append(peak)
                weights[here].append([p.astype(BF) for p in w])
            if 0 <= last < n:
                w = jnp.concatenate([p[step] for p in weights[last]], axis=0)
                pair = jnp.concatenate(fetched[last][2][2 * step : 2 * step + 2], axis=0)
                product = jnp.dot(w, pair, preferred_element_type=F32)
                acc = product if acc is None else acc + product
        if 0 <= last < n:
            h, b = blocks[last]
            peak, total = jnp.concatenate(peaks[last], axis=0), jnp.concatenate(totals[last], axis=0)
            out_refs[h][b * BS : (b + 1) * BS, :] = (acc * (1.0 / total)).astype(BF)
            lse = peak * EXP2 + jnp.log2(total)
            lses[h].append(jnp.transpose(jnp.broadcast_to(lse, (BS, HD)))[0:1, :])
            if b == HALF - 1:
                out_refs[h][ROWS:, :] = split3(jnp.concatenate(lses[h], axis=0))
            fetched[last] = scores[last] = weights[last] = None


def merge_kernel(keep, pairs, *refs):
    n_in = len(refs) - len(pairs)
    for n, members in enumerate(pairs):
        ins, out_ref = [refs[m] for m in members], refs[n_in + n]
        lses = [join3(r[ROWS:, :]) for r in ins]
        top = functools.reduce(jnp.maximum, lses)
        parts = [jnp.exp2(s - top) for s in lses]
        total = functools.reduce(jnp.add, parts)
        parts = [p / total for p in parts]
        for b in range(HALF):
            rows = slice(b * BS, (b + 1) * BS)
            acc = jnp.zeros((BS, HD), F32)
            for r, p in zip(ins, parts):
                acc = acc + jnp.transpose(jnp.broadcast_to(p[b : b + 1, :], (BS, HD))) * r[rows, :].astype(F32)
            out_ref[rows, :] = acc.astype(BF)
        if keep:
            out_ref[ROWS:, :] = split3(top + jnp.log2(total))


def unpack_kernel(in_ref, out_ref):
    for h in range(HEADS):
        out_ref[:, h * HD : (h + 1) * HD] = in_ref[h]


def call(kernel, outs, specs, *args, scratch=(), flops=0, moved=1 << 18):
    return pl.pallas_call(
        kernel,
        out_shape=outs,
        in_specs=specs,
        out_specs=jax.tree.map(lambda _: VMEM, outs),
        scratch_shapes=list(scratch),
        compiler_params=pltpu.CompilerParams(vmem_limit_bytes=24 << 20),
        cost_estimate=pl.CostEstimate(flops=flops, bytes_accessed=moved, transcendentals=0),
    )(*args)


def half_shape(rows=ROWS + EXTRA):
    return jax.ShapeDtypeStruct((rows, HD), BF)


def attend(columns, picks, queries, halves, kvs):
    return call(
        functools.partial(attend_kernel, halves, len(kvs)),
        [half_shape() for _ in halves],
        [SMEM, SMEM] + [VMEM] * (len(queries) + len(kvs)),
        columns, picks, *queries, *kvs,
        flops=len(halves) * (1 << 28), moved=4 << 20,
    )


def merge(keep, pairs, *ins):
    outs = [half_shape() if keep else half_shape(ROWS) for _ in pairs]
    return call(functools.partial(merge_kernel, keep, pairs), outs, [VMEM] * len(ins), *ins)


def picks_of(*halves):
    return jnp.concatenate([h[ROWS : ROWS + HALF] for h in halves], axis=0).astype(jnp.int32)


def shards(queries, keys, values, block_mask):
    x, z, c = lax.axis_index("x"), lax.axis_index("zh"), lax.axis_index("core")
    here_uly = lax.axis_index(("y", "zl"))
    head = jnp.minimum(here_uly, HEADS - 1).reshape(1).astype(jnp.int32)
    packed, picks = call(
        pack_kernel,
        (jax.ShapeDtypeStruct((NU, 3 * TOK, HD), BF), jax.ShapeDtypeStruct((2, EXTRA, HD), BF)),
        [SMEM, ANY, ANY, ANY, ANY],
        head, queries, keys, values, block_mask,
        scratch=[pltpu.VMEM(queries.shape, BF)] * 3
        + [pltpu.VMEM(block_mask.shape[1:], jnp.int32), pltpu.SemaphoreType.DMA((4,))],
    )
    got = lax.all_to_all(packed, ("y", "zl"), split_axis=0, concat_axis=0, tiled=True)
    kv_own = got[:, TOK:]
    q0 = jnp.concatenate([got[:, :TOK].reshape(2, ROWS, HD), picks], axis=1)

    kvs = [lax.all_gather(kv_own, ("x", "core"), axis=0, tiled=False)]
    columns = [(i // NC * NZ + z) * NC + i % NC for i in range(GROUPS)]
    columns = jnp.stack(columns).astype(jnp.int32)
    q1, q3 = shift(q0, "zh", 1), shift(q0, "zh", -1)
    q2a, q2b = shift(q1[0], "zh", 1), shift(q3[1], "zh", -1)

    o2a, o2b = attend(columns, picks_of(q2a, q2b), [q2a, q2b], ((0, None), (1, None)), kvs)
    via_a, via_b = shift(o2a, "zh", 1), shift(o2b, "zh", -1)
    o0a, o0b, o1a, o1b, o3a, o3b = attend(
        columns, picks_of(q0[0], q0[1], q1[0], q1[1], q3[0], q3[1]), [q0, q1, q3],
        ((0, 0), (0, 1), (1, 0), (1, 1), (2, 0), (2, 1)), kvs,
    )
    m1b, m3a = merge(True, ((0, 1), (2, 3)), o1b, via_b, o3a, via_a)
    back1 = shift(jnp.stack([o1a, m1b]), "zh", -1)
    back3 = shift(jnp.stack([m3a, o3b]), "zh", 1)
    whole = merge(False, ((0, 2, 4), (1, 3, 5)), o0a, o0b, back1[0], back1[1], back3[0], back3[1])
    whole = jnp.concatenate(whole, axis=0).reshape(NU, TOK, HD)
    home = lax.all_to_all(whole, ("y", "zl"), split_axis=0, concat_axis=0, tiled=True)
    return call(unpack_kernel, jax.ShapeDtypeStruct((TOK, HEADS * HD), BF), [VMEM], home)


def solution(mesh):
    fine = Mesh(mesh.devices.reshape(NX, NZ, NC, NU // 2, 2), AXES)
    tokens = P(AXES, None)
    placed = (tokens, tokens, tokens, P(None, AXES[:3], None))
    return jax.shard_map(shards, mesh=fine, in_specs=placed, out_specs=tokens, check_vma=False)
```

```python
import functools
import math

import jax
import jax.numpy as jnp
from jax import lax
from jax.experimental import pallas as pl
from jax.experimental.pallas import tpu as pltpu
from jax.sharding import Mesh, PartitionSpec as P

BF = jnp.bfloat16
F32 = jnp.float32
NX, NZ, NC, NU = 4, 4, 2, 16
HEADS, HD, BS, TOK = 12, 128, 128, 64
SEGB = 8
GROUPS = NX * NC
HALF = 4
ROWS = HALF * BS
EXTRA = 16
EXP2 = math.log2(math.e) / math.sqrt(HD)
AXES = ("x", "zh", "core", "y", "zl")
VMEM = pl.BlockSpec(memory_space=pltpu.VMEM)
SMEM = pl.BlockSpec(memory_space=pltpu.SMEM)
HBM = pl.BlockSpec(memory_space=pltpu.HBM)


def shift(field, axis, by):
    n = lax.axis_size(axis)
    return lax.ppermute(field, axis, [(i, (i + by) % n) for i in range(n)])


def pack_kernel(head_ref, q_hbm, k_hbm, v_hbm, mask_hbm, out_ref, picks_ref, q_ref, k_ref, v_ref, mask_ref, sems):
    pairs = ((mask_hbm.at[head_ref[0]], mask_ref), (q_hbm, q_ref), (k_hbm, k_ref), (v_hbm, v_ref))
    copies = [pltpu.make_async_copy(src, dst, sems.at[i]) for i, (src, dst) in enumerate(pairs)]
    for copy in copies:
        copy.start()
    for s in range(HEADS, NU):
        out_ref[s] = jnp.zeros((3 * TOK, HD), BF)
    copies[0].wait()
    live = mask_ref[...].astype(F32).astype(BF)
    cols = live.shape[1]
    i = lax.broadcasted_iota(jnp.int32, (cols, HD), 0)
    g = lax.broadcasted_iota(jnp.int32, (cols, HD), 1)
    weight = jnp.where(i // SEGB == g, i % SEGB, 0).astype(F32).astype(BF)
    picks = jnp.dot(live, weight, preferred_element_type=F32)
    pad = jnp.zeros((EXTRA - HALF, HD), F32)
    for half in range(2):
        picks_ref[half] = jnp.concatenate([picks[half * HALF : (half + 1) * HALF], pad], axis=0).astype(BF)
    for n, ref in enumerate((q_ref, k_ref, v_ref)):
        copies[n + 1].wait()
        for h in range(HEADS):
            out_ref[h, n * TOK : (n + 1) * TOK, :] = ref[:, h * HD : (h + 1) * HD]


def split3(lse):
    hi = lse.astype(BF).astype(F32)
    mid = (lse - hi).astype(BF).astype(F32)
    return jnp.concatenate([hi, mid, lse - hi - mid, jnp.zeros_like(hi)], axis=0).astype(BF)


def join3(rows):
    rows = rows.astype(F32)
    return rows[0:HALF] + rows[HALF : 2 * HALF] + rows[2 * HALF : 3 * HALF]


def attend_kernel(halves, n_kv, columns_ref, picks_ref, *refs):
    n_q = len(set(ref for ref, _ in halves))
    q_refs, kv_refs, out_refs = refs[:n_q], refs[n_q : n_q + n_kv], refs[n_q + n_kv :]
    groups = kv_refs if n_kv == GROUPS else [kv_refs[0].at[g] for g in range(GROUPS)]
    columns = [columns_ref[g] for g in range(GROUPS)]
    blocks = [(h, b) for h in range(len(halves)) for b in range(HALF)]
    n = len(blocks)
    fetched, scores, weights, peaks, totals = {}, {}, {}, {}, {}
    lses = [[] for _ in halves]
    for t in range(n + 2):
        ahead, here, last = t, t - 1, t - 2
        if ahead < n:
            h, b = blocks[ahead]
            ref, part = halves[h]
            q = (q_refs[ref] if part is None else q_refs[ref].at[part])[b * BS : (b + 1) * BS, :]
            keys, values = [], []
            for g in range(GROUPS):
                j = picks_ref[h * HALF + b, columns[g]]
                both = groups[g][pl.ds(2 * j, 2)]
                keys.append(both[:, :TOK, :].reshape(BS, HD))
                values.append(both[:, TOK:, :].reshape(BS, HD))
            fetched[ahead], scores[ahead] = (q, keys, values), []
        if 0 <= here < n:
            weights[here], peaks[here], totals[here] = [], [], []
        acc = None
        for step in range(4):
            if ahead < n:
                q, keys, _ = fetched[ahead]
                pair = jnp.concatenate(keys[2 * step : 2 * step + 2], axis=0)
                scores[ahead].append(
                    lax.dot_general(q, pair, (((1,), (1,)), ((), ())), preferred_element_type=F32)
                )
            if 0 <= here < n:
                rows = slice(step * BS // 4, (step + 1) * BS // 4)
                part = [s[rows] for s in scores[here]]
                peak = jnp.max(functools.reduce(jnp.maximum, part), axis=1, keepdims=True)
                w = [jnp.exp2((s - peak) * EXP2) for s in part]
                totals[here].append(jnp.sum(functools.reduce(jnp.add, w), axis=1, keepdims=True))
                peaks[here].append(peak)
                weights[here].append([p.astype(BF) for p in w])
            if 0 <= last < n:
                w = jnp.concatenate([p[step] for p in weights[last]], axis=0)
                pair = jnp.concatenate(fetched[last][2][2 * step : 2 * step + 2], axis=0)
                product = jnp.dot(w, pair, preferred_element_type=F32)
                acc = product if acc is None else acc + product
        if 0 <= last < n:
            h, b = blocks[last]
            peak, total = jnp.concatenate(peaks[last], axis=0), jnp.concatenate(totals[last], axis=0)
            out_refs[h][b * BS : (b + 1) * BS, :] = (acc * (1.0 / total)).astype(BF)
            lse = peak * EXP2 + jnp.log2(total)
            lses[h].append(jnp.transpose(jnp.broadcast_to(lse, (BS, HD)))[0:1, :])
            if b == HALF - 1:
                out_refs[h][ROWS:, :] = split3(jnp.concatenate(lses[h], axis=0))
            fetched[last] = scores[last] = weights[last] = None


def merge_kernel(keep, pairs, *refs):
    n_in = len(refs) - len(pairs)
    for n, members in enumerate(pairs):
        ins, out_ref = [refs[m] for m in members], refs[n_in + n]
        lses = [join3(r[ROWS:, :]) for r in ins]
        top = functools.reduce(jnp.maximum, lses)
        parts = [jnp.exp2(s - top) for s in lses]
        total = functools.reduce(jnp.add, parts)
        parts = [p / total for p in parts]
        for b in range(HALF):
            rows = slice(b * BS, (b + 1) * BS)
            acc = jnp.zeros((BS, HD), F32)
            for r, p in zip(ins, parts):
                acc = acc + jnp.transpose(jnp.broadcast_to(p[b : b + 1, :], (BS, HD))) * r[rows, :].astype(F32)
            out_ref[rows, :] = acc.astype(BF)
        if keep:
            out_ref[ROWS:, :] = split3(top + jnp.log2(total))


def unpack_kernel(in_ref, out_ref):
    for h in range(HEADS):
        out_ref[:, h * HD : (h + 1) * HD] = in_ref[h]


def call(kernel, outs, specs, *args, scratch=(), flops=0, moved=1 << 18):
    return pl.pallas_call(
        kernel,
        out_shape=outs,
        in_specs=specs,
        out_specs=jax.tree.map(lambda _: VMEM, outs),
        scratch_shapes=list(scratch),
        compiler_params=pltpu.CompilerParams(vmem_limit_bytes=24 << 20),
        cost_estimate=pl.CostEstimate(flops=flops, bytes_accessed=moved, transcendentals=0),
    )(*args)


def half_shape(rows=ROWS + EXTRA):
    return jax.ShapeDtypeStruct((rows, HD), BF)


def attend(columns, picks, queries, halves, kvs):
    return call(
        functools.partial(attend_kernel, halves, len(kvs)),
        [half_shape() for _ in halves],
        [SMEM, SMEM] + [VMEM] * (len(queries) + len(kvs)),
        columns, picks, *queries, *kvs,
        flops=len(halves) * (1 << 28), moved=4 << 20,
    )


def merge(keep, pairs, *ins):
    outs = [half_shape() if keep else half_shape(ROWS) for _ in pairs]
    return call(functools.partial(merge_kernel, keep, pairs), outs, [VMEM] * len(ins), *ins)


def picks_of(*halves):
    return jnp.concatenate([h[ROWS : ROWS + HALF] for h in halves], axis=0).astype(jnp.int32)


def shards(queries, keys, values, block_mask):
    x, z, c = lax.axis_index("x"), lax.axis_index("zh"), lax.axis_index("core")
    here_uly = lax.axis_index(("y", "zl"))
    head = jnp.minimum(here_uly, HEADS - 1).reshape(1).astype(jnp.int32)
    packed, picks = call(
        pack_kernel,
        (jax.ShapeDtypeStruct((NU, 3 * TOK, HD), BF), jax.ShapeDtypeStruct((2, EXTRA, HD), BF)),
        [SMEM, HBM, HBM, HBM, HBM],
        head, queries, keys, values, block_mask,
        scratch=[pltpu.VMEM(queries.shape, BF)] * 3
        + [pltpu.VMEM(block_mask.shape[1:], jnp.int32), pltpu.SemaphoreType.DMA((4,))],
    )
    got = lax.all_to_all(packed, ("y", "zl"), split_axis=0, concat_axis=0, tiled=True)
    kv_own = got[:, TOK:]
    q0 = jnp.concatenate([got[:, :TOK].reshape(2, ROWS, HD), picks], axis=1)

    kvs, columns = [], []
    for dx in (1, 3, 0, 2):
        near = kv_own if dx == 0 else shift(kv_own, "x", dx)
        kvs += [near, shift(near, "core", 1)]
        columns += [((x - dx) % NX * NZ + z) * NC + cc for cc in (c, 1 - c)]
    columns = jnp.stack(columns).astype(jnp.int32)
    q1, q3 = shift(q0, "zh", 1), shift(q0, "zh", -1)
    q2a, q2b = shift(q1[0], "zh", 1), shift(q3[1], "zh", -1)

    o2a, o2b = attend(columns, picks_of(q2a, q2b), [q2a, q2b], ((0, None), (1, None)), kvs)
    via_a, via_b = shift(o2a, "zh", 1), shift(o2b, "zh", -1)
    o0a, o0b, o1a, o1b, o3a, o3b = attend(
        columns, picks_of(q0[0], q0[1], q1[0], q1[1], q3[0], q3[1]), [q0, q1, q3],
        ((0, 0), (0, 1), (1, 0), (1, 1), (2, 0), (2, 1)), kvs,
    )
    m1b, m3a = merge(True, ((0, 1), (2, 3)), o1b, via_b, o3a, via_a)
    back1 = shift(jnp.stack([o1a, m1b]), "zh", -1)
    back3 = shift(jnp.stack([m3a, o3b]), "zh", 1)
    whole = merge(False, ((0, 2, 4), (1, 3, 5)), o0a, o0b, back1[0], back1[1], back3[0], back3[1])
    whole = jnp.concatenate(whole, axis=0).reshape(NU, TOK, HD)
    home = lax.all_to_all(whole, ("y", "zl"), split_axis=0, concat_axis=0, tiled=True)
    return call(unpack_kernel, jax.ShapeDtypeStruct((TOK, HEADS * HD), BF), [VMEM], home)


def solution(mesh):
    fine = Mesh(mesh.devices.reshape(NX, NZ, NC, NU // 2, 2), AXES)
    tokens = P(AXES, None)
    placed = (tokens, tokens, tokens, P(None, AXES[:3], None))
    return jax.shard_map(shards, mesh=fine, in_specs=placed, out_specs=tokens, check_vma=False)
```

```python
import functools
import math

import jax
import jax.numpy as jnp
from jax import lax
from jax.experimental import pallas as pl
from jax.experimental.pallas import tpu as pltpu
from jax.sharding import Mesh, PartitionSpec as P

BF = jnp.bfloat16
F32 = jnp.float32
NX, NZ, NC, NU = 4, 4, 2, 16
HEADS, HD, BS, TOK = 12, 128, 128, 64
SEGB = 8
GROUPS = NX * NC
HALF = 4
ROWS = HALF * BS
EXTRA = 16
EXP2 = math.log2(math.e) / math.sqrt(HD)
SHIFTS = (0, 1, 3, 2)
AXES = ("x", "zh", "core", "y", "zl")
VMEM = pl.BlockSpec(memory_space=pltpu.VMEM)
HBM = pl.BlockSpec(memory_space=pltpu.HBM)


def shift(field, axis, by):
    n = lax.axis_size(axis)
    return lax.ppermute(field, axis, [(i, (i + by) % n) for i in range(n)])


def pack_kernel(q_hbm, k_hbm, v_hbm, mask_hbm, out_ref, picks_ref, q_ref, k_ref, v_ref, mask_ref, sems):
    head = jnp.minimum(lax.axis_index("y") * 2 + lax.axis_index("zl"), HEADS - 1)
    pairs = ((q_hbm, q_ref), (k_hbm, k_ref), (v_hbm, v_ref), (mask_hbm.at[head], mask_ref))
    copies = [pltpu.make_async_copy(src, dst, sems.at[i]) for i, (src, dst) in enumerate(pairs)]
    for copy in copies:
        copy.start()
    for s in range(HEADS, NU):
        out_ref[s] = jnp.zeros((3 * TOK, HD), BF)
    for n, ref in enumerate((q_ref, k_ref, v_ref)):
        copies[n].wait()
        for h in range(HEADS):
            out_ref[h, n * TOK : (n + 1) * TOK, :] = ref[:, h * HD : (h + 1) * HD]
    copies[3].wait()
    live = mask_ref[...].astype(F32).astype(BF)
    cols = live.shape[1]
    i = lax.broadcasted_iota(jnp.int32, (cols, HD), 0)
    g = lax.broadcasted_iota(jnp.int32, (cols, HD), 1)
    weight = jnp.where(i // SEGB == g, i % SEGB, 0).astype(F32).astype(BF)
    picks = jnp.dot(live, weight, preferred_element_type=F32)
    pad = jnp.zeros((EXTRA - HALF, HD), F32)
    for half in range(2):
        picks_ref[half] = jnp.concatenate([picks[half * HALF : (half + 1) * HALF], pad], axis=0).astype(BF)


def split3(lse):
    hi = lse.astype(BF).astype(F32)
    mid = (lse - hi).astype(BF).astype(F32)
    return jnp.concatenate([hi, mid, lse - hi - mid, jnp.zeros_like(hi)], axis=0).astype(BF)


def join3(rows):
    rows = rows.astype(F32)
    return rows[0:HALF] + rows[HALF : 2 * HALF] + rows[2 * HALF : 3 * HALF]


def attend_kernel(halves, n_q, kv_slots, out_slots, *refs):
    def view(group, slot):
        return group[slot[0]] if slot[1] is None else group[slot[0]].at[slot[1]]

    n_kv, n_out = max(r for r, _ in kv_slots) + 1, max(r for r, _ in out_slots) + 1
    q_refs, kv_refs, out_refs = refs[:n_q], refs[n_q : n_q + n_kv], refs[n_q + n_kv : n_q + n_kv + n_out]
    flat_ref, picks_ref, sem = refs[n_q + n_kv + n_out :]
    for h, slot in enumerate(halves):
        flat_ref[h * SEGB : (h + 1) * SEGB, :] = view(q_refs, slot)[ROWS:, :].astype(F32)[:SEGB].astype(jnp.int32)
    fetch = pltpu.make_async_copy(flat_ref, picks_ref, sem)
    fetch.start()
    x, z, c = lax.axis_index("x"), lax.axis_index("zh"), lax.axis_index("core")
    columns = [((x + NX - dx) % NX * NZ + z) * NC + cc for dx in SHIFTS for cc in (c, 1 - c)]
    groups = [view(kv_refs, slot) for slot in kv_slots]
    outs = [view(out_refs, slot) for slot in out_slots]
    fetch.wait()
    blocks = [(h, b) for h in range(len(halves)) for b in range(HALF)]
    n = len(blocks)
    fetched, scores, weights, peaks, totals = {}, {}, {}, {}, {}
    lses = [[] for _ in halves]
    for t in range(n + 2):
        ahead, here, last = t, t - 1, t - 2
        if ahead < n:
            h, b = blocks[ahead]
            q = view(q_refs, halves[h])[b * BS : (b + 1) * BS, :]
            keys, values = [], []
            for g in range(GROUPS):
                j = picks_ref[h * SEGB + b, columns[g]]
                both = groups[g][pl.ds(2 * j, 2)]
                keys.append(both[:, :TOK, :].reshape(BS, HD))
                values.append(both[:, TOK:, :].reshape(BS, HD))
            fetched[ahead], scores[ahead] = (q, keys, values), []
        if 0 <= here < n:
            weights[here], peaks[here], totals[here] = [], [], []
        acc = None
        for step in range(4):
            if ahead < n:
                q, keys, _ = fetched[ahead]
                pair = jnp.concatenate(keys[2 * step : 2 * step + 2], axis=0)
                scores[ahead].append(
                    lax.dot_general(q, pair, (((1,), (1,)), ((), ())), preferred_element_type=F32)
                )
            if 0 <= here < n:
                rows = slice(step * BS // 4, (step + 1) * BS // 4)
                part = [s[rows] for s in scores[here]]
                peak = jnp.max(functools.reduce(jnp.maximum, part), axis=1, keepdims=True)
                w = [jnp.exp2((s - peak) * EXP2) for s in part]
                totals[here].append(jnp.sum(functools.reduce(jnp.add, w), axis=1, keepdims=True))
                peaks[here].append(peak)
                weights[here].append([p.astype(BF) for p in w])
            if 0 <= last < n:
                w = jnp.concatenate([p[step] for p in weights[last]], axis=0)
                pair = jnp.concatenate(fetched[last][2][2 * step : 2 * step + 2], axis=0)
                product = jnp.dot(w, pair, preferred_element_type=F32)
                acc = product if acc is None else acc + product
        if 0 <= last < n:
            h, b = blocks[last]
            peak, total = jnp.concatenate(peaks[last], axis=0), jnp.concatenate(totals[last], axis=0)
            outs[h][b * BS : (b + 1) * BS, :] = (acc * (1.0 / total)).astype(BF)
            lse = peak * EXP2 + jnp.log2(total)
            lses[h].append(jnp.transpose(jnp.broadcast_to(lse, (BS, HD)))[0:1, :])
            if b == HALF - 1:
                outs[h][ROWS:, :] = split3(jnp.concatenate(lses[h], axis=0))
            fetched[last] = scores[last] = weights[last] = None


def merge_halves(ins, out_ref, first, keep):
    lses = [join3(r[ROWS:, :]) for r in ins]
    top = functools.reduce(jnp.maximum, lses)
    parts = [jnp.exp2(s - top) for s in lses]
    total = functools.reduce(jnp.add, parts)
    parts = [p / total for p in parts]
    for b in range(HALF):
        rows = slice(b * BS, (b + 1) * BS)
        acc = jnp.zeros((BS, HD), F32)
        for r, p in zip(ins, parts):
            acc = acc + jnp.transpose(jnp.broadcast_to(p[b : b + 1, :], (BS, HD))) * r[rows, :].astype(F32)
        out_ref[first + b * BS : first + (b + 1) * BS, :] = acc.astype(BF)
    if keep:
        out_ref[ROWS:, :] = split3(top + jnp.log2(total))


def pass_kernel(o1_ref, o3_ref, via_a_ref, via_b_ref, out1_ref, out3_ref):
    out1_ref[0] = o1_ref[0]
    merge_halves([o1_ref.at[1], via_b_ref], out1_ref.at[1], 0, True)
    merge_halves([o3_ref.at[0], via_a_ref], out3_ref.at[0], 0, True)
    out3_ref[1] = o3_ref[1]


def final_kernel(a_ref, b_ref, c_ref, out_ref):
    for half in range(2):
        merge_halves([r.at[half] for r in (a_ref, b_ref, c_ref)], out_ref, half * ROWS, False)


def unpack_kernel(in_ref, out_ref):
    for h in range(HEADS):
        out_ref[:, h * HD : (h + 1) * HD] = in_ref[h]


def call(kernel, outs, specs, *args, scratch=(), flops=0, moved=1 << 18, vmem=24):
    return pl.pallas_call(
        kernel,
        out_shape=outs,
        in_specs=specs,
        out_specs=jax.tree.map(lambda _: VMEM, outs),
        scratch_shapes=list(scratch),
        compiler_params=pltpu.CompilerParams(vmem_limit_bytes=vmem << 20),
        cost_estimate=pl.CostEstimate(flops=flops, bytes_accessed=moved, transcendentals=0),
    )(*args)


def half_shape():
    return jax.ShapeDtypeStruct((ROWS + EXTRA, HD), BF)


def chunk_shape():
    return jax.ShapeDtypeStruct((2, ROWS + EXTRA, HD), BF)


def attend(queries, halves, outs, out_slots, kvs, kv_slots):
    n = len(halves)
    return call(
        functools.partial(attend_kernel, halves, len(queries), kv_slots, out_slots),
        outs, [VMEM] * (len(queries) + len(kvs)), *queries, *kvs,
        scratch=[pltpu.VMEM((n * SEGB, HD), jnp.int32), pltpu.SMEM((n * SEGB, HD), jnp.int32), pltpu.SemaphoreType.DMA],
        flops=n * (1 << 28), moved=4 << 20,
    )


def shards(queries, keys, values, block_mask):
    packed, picks = call(
        pack_kernel,
        (jax.ShapeDtypeStruct((NU, 3 * TOK, HD), BF), jax.ShapeDtypeStruct((2, EXTRA, HD), BF)),
        [HBM] * 4, queries, keys, values, block_mask,
        scratch=[pltpu.VMEM(queries.shape, BF)] * 3
        + [pltpu.VMEM(block_mask.shape[1:], jnp.int32), pltpu.SemaphoreType.DMA((4,))],
        vmem=60,
    )
    got = lax.all_to_all(packed, ("y", "zl"), split_axis=0, concat_axis=0, tiled=True)
    k0 = got[:, TOK:]
    q0 = jnp.concatenate([got[:, :TOK].reshape(2, ROWS, HD), picks], axis=1)

    k1, k3, k2 = (shift(k0, "x", dx) for dx in SHIFTS[1:])
    q1, q3 = shift(q0, "zh", 1), shift(q0, "zh", -1)
    c0 = shift(k0, "core", 1)
    q2a, q2b = shift(q1[0], "zh", 1), shift(q3[1], "zh", -1)
    c13 = shift(jnp.stack([k1, k3]), "core", 1)
    c2 = shift(k2, "core", 1)
    kvs = [k0, c0, k1, k3, c13, k2, c2]
    slots = ((0, None), (1, None), (2, None), (4, 0), (3, None), (4, 1), (5, None), (6, None))

    o2a, o2b = attend([q2a, q2b], ((0, None), (1, None)), [half_shape()] * 2, ((0, None), (1, None)), kvs, slots)
    via_a, via_b = shift(o2a, "zh", 1), shift(o2b, "zh", -1)
    four = ((0, 0), (0, 1), (1, 0), (1, 1))
    o1, o3 = attend([q1, q3], four, [chunk_shape()] * 2, four, kvs, slots)
    m1, m3 = call(pass_kernel, [chunk_shape()] * 2, [VMEM] * 4, o1, o3, via_a, via_b)
    m1, m3, q0 = lax.optimization_barrier((m1, m3, q0))
    back1, back3 = shift(m1, "zh", -1), shift(m3, "zh", 1)
    (o0,) = attend([q0], four[:2], [chunk_shape()], four[:2], kvs, slots)
    whole = call(final_kernel, jax.ShapeDtypeStruct((NU * TOK, HD), BF), [VMEM] * 3, o0, back1, back3)
    home = lax.all_to_all(whole.reshape(NU, TOK, HD), ("y", "zl"), split_axis=0, concat_axis=0, tiled=True)
    return call(unpack_kernel, jax.ShapeDtypeStruct((TOK, HEADS * HD), BF), [VMEM], home)


def solution(mesh):
    fine = Mesh(mesh.devices.reshape(NX, NZ, NC, NU // 2, 2), AXES)
    tokens = P(AXES, None)
    placed = (tokens, tokens, tokens, P(None, AXES[:3], None))
    return jax.shard_map(shards, mesh=fine, in_specs=placed, out_specs=tokens, check_vma=False)
```

```python
import functools
import math

import jax
import jax.numpy as jnp
from jax import lax
from jax.experimental import pallas as pl
from jax.experimental.pallas import tpu as pltpu
from jax.sharding import Mesh, PartitionSpec as P

BF = jnp.bfloat16
F32 = jnp.float32
NX, NZ, NC, NU = 4, 4, 2, 16
HEADS, HD, BS, TOK = 12, 128, 128, 64
SEGB = 8
GROUPS = NX * NC
HALF = 4
ROWS = HALF * BS
EXTRA = 16
EXP2 = math.log2(math.e) / math.sqrt(HD)
SHIFTS = (0, 1, 3, 2)
AXES = ("x", "zh", "core", "y", "zl")
VMEM = pl.BlockSpec(memory_space=pltpu.VMEM)
HBM = pl.BlockSpec(memory_space=pltpu.HBM)


def shift(field, axis, by):
    n = lax.axis_size(axis)
    return lax.ppermute(field, axis, [(i, (i + by) % n) for i in range(n)])


def pack_kernel(q_hbm, k_hbm, v_hbm, mask_hbm, out_ref, picks_ref, q_ref, k_ref, v_ref, mask_ref, sems):
    head = jnp.minimum(lax.axis_index("y") * 2 + lax.axis_index("zl"), HEADS - 1)
    pairs = ((q_hbm, q_ref), (k_hbm, k_ref), (v_hbm, v_ref), (mask_hbm.at[head], mask_ref))
    copies = [pltpu.make_async_copy(src, dst, sems.at[i]) for i, (src, dst) in enumerate(pairs)]
    for copy in copies:
        copy.start()
    for s in range(HEADS, NU):
        out_ref[s] = jnp.zeros((3 * TOK, HD), BF)
    for n, ref in enumerate((q_ref, k_ref, v_ref)):
        copies[n].wait()
        for h in range(HEADS):
            out_ref[h, n * TOK : (n + 1) * TOK, :] = ref[:, h * HD : (h + 1) * HD]
    copies[3].wait()
    live = mask_ref[...].astype(F32).astype(BF)
    cols = live.shape[1]
    i = lax.broadcasted_iota(jnp.int32, (cols, HD), 0)
    g = lax.broadcasted_iota(jnp.int32, (cols, HD), 1)
    weight = jnp.where(i // SEGB == g, i % SEGB, 0).astype(F32).astype(BF)
    picks = jnp.dot(live, weight, preferred_element_type=F32)
    pad = jnp.zeros((EXTRA - HALF, HD), F32)
    for half in range(2):
        picks_ref[half] = jnp.concatenate([picks[half * HALF : (half + 1) * HALF], pad], axis=0).astype(BF)


def split3(lse):
    hi = lse.astype(BF).astype(F32)
    mid = (lse - hi).astype(BF).astype(F32)
    return jnp.concatenate([hi, mid, lse - hi - mid, jnp.zeros_like(hi)], axis=0).astype(BF)


def join3(rows):
    rows = rows.astype(F32)
    return rows[0:HALF] + rows[HALF : 2 * HALF] + rows[2 * HALF : 3 * HALF]


def attend_kernel(halves, n_q, kv_slots, out_slots, *refs):
    def view(group, slot):
        return group[slot[0]] if slot[1] is None else group[slot[0]].at[slot[1]]

    n_kv, n_out = max(r for r, _ in kv_slots) + 1, max(r for r, _ in out_slots) + 1
    q_refs, kv_refs, out_refs = refs[:n_q], refs[n_q : n_q + n_kv], refs[n_q + n_kv : n_q + n_kv + n_out]
    flat_ref, picks_ref, sem = refs[n_q + n_kv + n_out :]
    for h, slot in enumerate(halves):
        flat_ref[h * SEGB : (h + 1) * SEGB, :] = view(q_refs, slot)[ROWS:, :].astype(F32)[:SEGB].astype(jnp.int32)
    fetch = pltpu.make_async_copy(flat_ref, picks_ref, sem)
    fetch.start()
    x, z, c = lax.axis_index("x"), lax.axis_index("zh"), lax.axis_index("core")
    columns = [((x + NX - dx) % NX * NZ + z) * NC + cc for dx in SHIFTS for cc in (c, 1 - c)]
    groups = [view(kv_refs, slot) for slot in kv_slots]
    outs = [view(out_refs, slot) for slot in out_slots]
    fetch.wait()
    blocks = [(h, b) for h in range(len(halves)) for b in range(HALF)]
    n = len(blocks)
    fetched, scores, weights, peaks, totals = {}, {}, {}, {}, {}
    lses = [[] for _ in halves]
    for t in range(n + 2):
        ahead, here, last = t, t - 1, t - 2
        if ahead < n:
            h, b = blocks[ahead]
            q = view(q_refs, halves[h])[b * BS : (b + 1) * BS, :]
            keys, values = [], []
            for g in range(GROUPS):
                j = picks_ref[h * SEGB + b, columns[g]]
                both = groups[g][pl.ds(2 * j, 2)]
                keys.append(both[:, :TOK, :].reshape(BS, HD))
                values.append(both[:, TOK:, :].reshape(BS, HD))
            fetched[ahead], scores[ahead] = (q, keys, values), []
        if 0 <= here < n:
            weights[here], peaks[here], totals[here] = [], [], []
        acc = None
        for step in range(4):
            if ahead < n:
                q, keys, _ = fetched[ahead]
                pair = jnp.concatenate(keys[2 * step : 2 * step + 2], axis=0)
                scores[ahead].append(
                    lax.dot_general(q, pair, (((1,), (1,)), ((), ())), preferred_element_type=F32)
                )
            if 0 <= here < n:
                rows = slice(step * BS // 4, (step + 1) * BS // 4)
                part = [s[rows] for s in scores[here]]
                peak = jnp.max(functools.reduce(jnp.maximum, part), axis=1, keepdims=True)
                w = [jnp.exp2((s - peak) * EXP2) for s in part]
                totals[here].append(jnp.sum(functools.reduce(jnp.add, w), axis=1, keepdims=True))
                peaks[here].append(peak)
                weights[here].append([p.astype(BF) for p in w])
            if 0 <= last < n:
                w = jnp.concatenate([p[step] for p in weights[last]], axis=0)
                pair = jnp.concatenate(fetched[last][2][2 * step : 2 * step + 2], axis=0)
                product = jnp.dot(w, pair, preferred_element_type=F32)
                acc = product if acc is None else acc + product
        if 0 <= last < n:
            h, b = blocks[last]
            peak, total = jnp.concatenate(peaks[last], axis=0), jnp.concatenate(totals[last], axis=0)
            outs[h][b * BS : (b + 1) * BS, :] = (acc * (1.0 / total)).astype(BF)
            lse = peak * EXP2 + jnp.log2(total)
            lses[h].append(jnp.transpose(jnp.broadcast_to(lse, (BS, HD)))[0:1, :])
            if b == HALF - 1:
                outs[h][ROWS:, :] = split3(jnp.concatenate(lses[h], axis=0))
            fetched[last] = scores[last] = weights[last] = None


def merge_halves(ins, out_ref, first, keep):
    lses = [join3(r[ROWS:, :]) for r in ins]
    top = functools.reduce(jnp.maximum, lses)
    parts = [jnp.exp2(s - top) for s in lses]
    total = functools.reduce(jnp.add, parts)
    parts = [p / total for p in parts]
    for b in range(HALF):
        rows = slice(b * BS, (b + 1) * BS)
        acc = jnp.zeros((BS, HD), F32)
        for r, p in zip(ins, parts):
            acc = acc + jnp.transpose(jnp.broadcast_to(p[b : b + 1, :], (BS, HD))) * r[rows, :].astype(F32)
        out_ref[first + b * BS : first + (b + 1) * BS, :] = acc.astype(BF)
    if keep:
        out_ref[ROWS:, :] = split3(top + jnp.log2(total))


def pass_kernel(o1_ref, o3_ref, via_a_ref, via_b_ref, out1_ref, out3_ref):
    out1_ref[0] = o1_ref[0]
    merge_halves([o1_ref.at[1], via_b_ref], out1_ref.at[1], 0, True)
    merge_halves([o3_ref.at[0], via_a_ref], out3_ref.at[0], 0, True)
    out3_ref[1] = o3_ref[1]


def final_kernel(a_ref, b_ref, c_ref, out_ref):
    for half in range(2):
        merge_halves([r.at[half] for r in (a_ref, b_ref, c_ref)], out_ref, half * ROWS, False)


def unpack_kernel(in_ref, out_ref):
    for h in range(HEADS):
        out_ref[:, h * HD : (h + 1) * HD] = in_ref[h]


def call(kernel, outs, specs, *args, scratch=(), flops=0, moved=1 << 18, vmem=24):
    return pl.pallas_call(
        kernel,
        out_shape=outs,
        in_specs=specs,
        out_specs=jax.tree.map(lambda _: VMEM, outs),
        scratch_shapes=list(scratch),
        compiler_params=pltpu.CompilerParams(vmem_limit_bytes=vmem << 20),
        cost_estimate=pl.CostEstimate(flops=flops, bytes_accessed=moved, transcendentals=0),
    )(*args)


def half_shape():
    return jax.ShapeDtypeStruct((ROWS + EXTRA, HD), BF)


def chunk_shape():
    return jax.ShapeDtypeStruct((2, ROWS + EXTRA, HD), BF)


def attend(queries, halves, outs, out_slots, kvs, kv_slots):
    n = len(halves)
    return call(
        functools.partial(attend_kernel, halves, len(queries), kv_slots, out_slots),
        outs, [VMEM] * (len(queries) + len(kvs)), *queries, *kvs,
        scratch=[pltpu.VMEM((n * SEGB, HD), jnp.int32), pltpu.SMEM((n * SEGB, HD), jnp.int32), pltpu.SemaphoreType.DMA],
        flops=n * (1 << 28), moved=4 << 20,
    )


def shards(queries, keys, values, block_mask):
    packed, picks = call(
        pack_kernel,
        (jax.ShapeDtypeStruct((NU, 3 * TOK, HD), BF), jax.ShapeDtypeStruct((2, EXTRA, HD), BF)),
        [HBM] * 4, queries, keys, values, block_mask,
        scratch=[pltpu.VMEM(queries.shape, BF)] * 3
        + [pltpu.VMEM(block_mask.shape[1:], jnp.int32), pltpu.SemaphoreType.DMA((4,))],
        vmem=60,
    )
    got = lax.all_to_all(packed, ("y", "zl"), split_axis=0, concat_axis=0, tiled=True)
    k0 = got[:, TOK:]
    q0 = jnp.concatenate([got[:, :TOK].reshape(2, ROWS, HD), picks], axis=1)

    k1, k3, k2 = (shift(k0, "x", dx) for dx in SHIFTS[1:])
    q1, q3 = shift(q0, "zh", 1), shift(q0, "zh", -1)
    q1, q3, k0, k1, k3, k2 = lax.optimization_barrier((q1, q3, k0, k1, k3, k2))
    c0 = shift(k0, "core", 1)
    q2a, q2b = shift(q1[0], "zh", 1), shift(q3[1], "zh", -1)
    near = jnp.stack([k1, k3, k2])
    far = shift(near, "core", 1)
    kvs = [k0, c0, near, far]
    slots = ((0, None), (1, None), (2, 0), (3, 0), (2, 1), (3, 1), (2, 2), (3, 2))

    o2a, o2b = attend([q2a, q2b], ((0, None), (1, None)), [half_shape()] * 2, ((0, None), (1, None)), kvs, slots)
    via_a, via_b = shift(o2a, "zh", 1), shift(o2b, "zh", -1)
    four = ((0, 0), (0, 1), (1, 0), (1, 1))
    o1, o3 = attend([q1, q3], four, [chunk_shape()] * 2, four, kvs, slots)
    m1, m3 = call(pass_kernel, [chunk_shape()] * 2, [VMEM] * 4, o1, o3, via_a, via_b)
    m1, m3, q0 = lax.optimization_barrier((m1, m3, q0))
    back1, back3 = shift(m1, "zh", -1), shift(m3, "zh", 1)
    (o0,) = attend([q0], four[:2], [chunk_shape()], four[:2], kvs, slots)
    whole = call(final_kernel, jax.ShapeDtypeStruct((NU * TOK, HD), BF), [VMEM] * 3, o0, back1, back3)
    home = lax.all_to_all(whole.reshape(NU, TOK, HD), ("y", "zl"), split_axis=0, concat_axis=0, tiled=True)
    return call(unpack_kernel, jax.ShapeDtypeStruct((TOK, HEADS * HD), BF), [VMEM], home)


def solution(mesh):
    fine = Mesh(mesh.devices.reshape(NX, NZ, NC, NU // 2, 2), AXES)
    tokens = P(AXES, None)
    placed = (tokens, tokens, tokens, P(None, AXES[:3], None))
    return jax.shard_map(shards, mesh=fine, in_specs=placed, out_specs=tokens, check_vma=False)
```

```python
import functools
import math

import jax
import jax.numpy as jnp
from jax import lax
from jax.experimental import pallas as pl
from jax.experimental.pallas import tpu as pltpu
from jax.sharding import Mesh, PartitionSpec as P

BF = jnp.bfloat16
F32 = jnp.float32
NX, NZ, NC, NU = 4, 4, 2, 16
HEADS, HD, BS, TOK = 12, 128, 128, 64
SEGB = 8
GROUPS = NX * NC
HALF = 4
ROWS = HALF * BS
EXTRA = 16
EXP2 = math.log2(math.e) / math.sqrt(HD)
SHIFTS = (0, 1, 3, 2)
AXES = ("x", "zh", "core", "y", "zl")
VMEM = pl.BlockSpec(memory_space=pltpu.VMEM)
HBM = pl.BlockSpec(memory_space=pltpu.HBM)


def shift(field, axis, by):
    n = lax.axis_size(axis)
    return lax.ppermute(field, axis, [(i, (i + by) % n) for i in range(n)])


def pack_kernel(q_hbm, k_hbm, v_hbm, mask_hbm, out_ref, picks_ref, q_ref, k_ref, v_ref, mask_ref, sems):
    head = jnp.minimum(lax.axis_index("y") * 2 + lax.axis_index("zl"), HEADS - 1)
    pairs = ((q_hbm, q_ref), (k_hbm, k_ref), (v_hbm, v_ref), (mask_hbm.at[head], mask_ref))
    copies = [pltpu.make_async_copy(src, dst, sems.at[i]) for i, (src, dst) in enumerate(pairs)]
    for copy in copies:
        copy.start()
    for s in range(HEADS, NU):
        out_ref[s] = jnp.zeros((3 * TOK, HD), BF)
    for n, ref in enumerate((q_ref, k_ref, v_ref)):
        copies[n].wait()
        for h in range(HEADS):
            out_ref[h, n * TOK : (n + 1) * TOK, :] = ref[:, h * HD : (h + 1) * HD]
    copies[3].wait()
    live = mask_ref[...].astype(F32).astype(BF)
    cols = live.shape[1]
    i = lax.broadcasted_iota(jnp.int32, (cols, HD), 0)
    g = lax.broadcasted_iota(jnp.int32, (cols, HD), 1)
    weight = jnp.where(i // SEGB == g, i % SEGB, 0).astype(F32).astype(BF)
    picks = jnp.dot(live, weight, preferred_element_type=F32)
    pad = jnp.zeros((EXTRA - HALF, HD), F32)
    for half in range(2):
        picks_ref[half] = jnp.concatenate([picks[half * HALF : (half + 1) * HALF], pad], axis=0).astype(BF)


def split3(lse):
    hi = lse.astype(BF).astype(F32)
    mid = (lse - hi).astype(BF).astype(F32)
    return jnp.concatenate([hi, mid, lse - hi - mid, jnp.zeros_like(hi)], axis=0).astype(BF)


def join3(rows):
    rows = rows.astype(F32)
    return rows[0:HALF] + rows[HALF : 2 * HALF] + rows[2 * HALF : 3 * HALF]


def attend_kernel(halves, n_q, kv_slots, out_slots, *refs):
    def view(group, slot):
        return group[slot[0]] if slot[1] is None else group[slot[0]].at[slot[1]]

    n_kv, n_out = max(r for r, _ in kv_slots) + 1, max(r for r, _ in out_slots) + 1
    q_refs, kv_refs, out_refs = refs[:n_q], refs[n_q : n_q + n_kv], refs[n_q + n_kv : n_q + n_kv + n_out]
    flat_ref, picks_ref, sem = refs[n_q + n_kv + n_out :]
    for h, slot in enumerate(halves):
        flat_ref[h * SEGB : (h + 1) * SEGB, :] = view(q_refs, slot)[ROWS:, :].astype(F32)[:SEGB].astype(jnp.int32)
    fetch = pltpu.make_async_copy(flat_ref, picks_ref, sem)
    fetch.start()
    x, z, c = lax.axis_index("x"), lax.axis_index("zh"), lax.axis_index("core")
    columns = [((x + NX - dx) % NX * NZ + z) * NC + cc for dx in SHIFTS for cc in (c, 1 - c)]
    groups = [view(kv_refs, slot) for slot in kv_slots]
    outs = [view(out_refs, slot) for slot in out_slots]
    fetch.wait()
    blocks = [(h, b) for h in range(len(halves)) for b in range(HALF)]
    n = len(blocks)
    fetched, scores, weights, peaks, totals = {}, {}, {}, {}, {}
    lses = [[] for _ in halves]
    for t in range(n + 2):
        ahead, here, last = t, t - 1, t - 2
        if ahead < n:
            h, b = blocks[ahead]
            q = view(q_refs, halves[h])[b * BS : (b + 1) * BS, :]
            keys, values = [], []
            for g in range(GROUPS):
                j = picks_ref[h * SEGB + b, columns[g]]
                both = groups[g][pl.ds(2 * j, 2)]
                keys.append(both[:, :TOK, :].reshape(BS, HD))
                values.append(both[:, TOK:, :].reshape(BS, HD))
            fetched[ahead], scores[ahead] = (q, keys, values), []
        if 0 <= here < n:
            weights[here], peaks[here], totals[here] = [], [], []
        acc = None
        for step in range(4):
            if ahead < n:
                q, keys, _ = fetched[ahead]
                pair = jnp.concatenate(keys[2 * step : 2 * step + 2], axis=0)
                scores[ahead].append(
                    lax.dot_general(q, pair, (((1,), (1,)), ((), ())), preferred_element_type=F32)
                )
            if 0 <= here < n:
                rows = slice(step * BS // 4, (step + 1) * BS // 4)
                part = [s[rows] for s in scores[here]]
                peak = jnp.max(functools.reduce(jnp.maximum, part), axis=1, keepdims=True)
                w = [jnp.exp2((s - peak) * EXP2) for s in part]
                totals[here].append(jnp.sum(functools.reduce(jnp.add, w), axis=1, keepdims=True))
                peaks[here].append(peak)
                weights[here].append([p.astype(BF) for p in w])
            if 0 <= last < n:
                w = jnp.concatenate([p[step] for p in weights[last]], axis=0)
                pair = jnp.concatenate(fetched[last][2][2 * step : 2 * step + 2], axis=0)
                product = jnp.dot(w, pair, preferred_element_type=F32)
                acc = product if acc is None else acc + product
        if 0 <= last < n:
            h, b = blocks[last]
            peak, total = jnp.concatenate(peaks[last], axis=0), jnp.concatenate(totals[last], axis=0)
            outs[h][b * BS : (b + 1) * BS, :] = (acc * (1.0 / total)).astype(BF)
            lse = peak * EXP2 + jnp.log2(total)
            lses[h].append(jnp.transpose(jnp.broadcast_to(lse, (BS, HD)))[0:1, :])
            if b == HALF - 1:
                outs[h][ROWS:, :] = split3(jnp.concatenate(lses[h], axis=0))
            fetched[last] = scores[last] = weights[last] = None


def merge_halves(ins, out_ref, first, keep):
    lses = [join3(r[ROWS:, :]) for r in ins]
    top = functools.reduce(jnp.maximum, lses)
    parts = [jnp.exp2(s - top) for s in lses]
    total = functools.reduce(jnp.add, parts)
    parts = [p / total for p in parts]
    for b in range(HALF):
        rows = slice(b * BS, (b + 1) * BS)
        acc = jnp.zeros((BS, HD), F32)
        for r, p in zip(ins, parts):
            acc = acc + jnp.transpose(jnp.broadcast_to(p[b : b + 1, :], (BS, HD))) * r[rows, :].astype(F32)
        out_ref[first + b * BS : first + (b + 1) * BS, :] = acc.astype(BF)
    if keep:
        out_ref[ROWS:, :] = split3(top + jnp.log2(total))


def pass_kernel(o1_ref, o3_ref, via_a_ref, via_b_ref, out1_ref, out3_ref):
    out1_ref[0] = o1_ref[0]
    merge_halves([o1_ref.at[1], via_b_ref], out1_ref.at[1], 0, True)
    merge_halves([o3_ref.at[0], via_a_ref], out3_ref.at[0], 0, True)
    out3_ref[1] = o3_ref[1]


def final_kernel(a_ref, b_ref, c_ref, out_ref):
    for half in range(2):
        merge_halves([r.at[half] for r in (a_ref, b_ref, c_ref)], out_ref, half * ROWS, False)


def unpack_kernel(in_ref, out_ref):
    for h in range(HEADS):
        out_ref[:, h * HD : (h + 1) * HD] = in_ref[h]


def call(kernel, outs, specs, *args, scratch=(), flops=0, moved=1 << 18, vmem=24):
    return pl.pallas_call(
        kernel,
        out_shape=outs,
        in_specs=specs,
        out_specs=jax.tree.map(lambda _: VMEM, outs),
        scratch_shapes=list(scratch),
        compiler_params=pltpu.CompilerParams(vmem_limit_bytes=vmem << 20),
        cost_estimate=pl.CostEstimate(flops=flops, bytes_accessed=moved, transcendentals=0),
    )(*args)


def half_shape():
    return jax.ShapeDtypeStruct((ROWS + EXTRA, HD), BF)


def chunk_shape():
    return jax.ShapeDtypeStruct((2, ROWS + EXTRA, HD), BF)


def attend(queries, halves, outs, out_slots, kvs, kv_slots):
    n = len(halves)
    return call(
        functools.partial(attend_kernel, halves, len(queries), kv_slots, out_slots),
        outs, [VMEM] * (len(queries) + len(kvs)), *queries, *kvs,
        scratch=[pltpu.VMEM((n * SEGB, HD), jnp.int32), pltpu.SMEM((n * SEGB, HD), jnp.int32), pltpu.SemaphoreType.DMA],
        flops=n * (1 << 28), moved=4 << 20,
    )


def shards(queries, keys, values, block_mask):
    packed, picks = call(
        pack_kernel,
        (jax.ShapeDtypeStruct((NU, 3 * TOK, HD), BF), jax.ShapeDtypeStruct((2, EXTRA, HD), BF)),
        [HBM] * 4, queries, keys, values, block_mask,
        scratch=[pltpu.VMEM(queries.shape, BF)] * 3
        + [pltpu.VMEM(block_mask.shape[1:], jnp.int32), pltpu.SemaphoreType.DMA((4,))],
        vmem=60,
    )
    got = lax.all_to_all(packed, ("y", "zl"), split_axis=0, concat_axis=0, tiled=True)
    k0 = got[:, TOK:]
    q0 = jnp.concatenate([got[:, :TOK].reshape(2, ROWS, HD), picks], axis=1)

    k1, k3, k2 = (shift(k0, "x", dx) for dx in SHIFTS[1:])
    q1, q3 = shift(q0, "zh", 1), shift(q0, "zh", -1)
    q2a, q2b = shift(q1[0], "zh", 1), shift(q3[1], "zh", -1)
    k1, k3, k2, q2a, q2b = lax.optimization_barrier((k1, k3, k2, q2a, q2b))
    near = jnp.stack([k0, k1, k3, k2])
    far = shift(near, "core", 1)
    kvs = [near, far]
    slots = tuple((ref, n) for n in range(NX) for ref in range(NC))

    o2a, o2b = attend([q2a, q2b], ((0, None), (1, None)), [half_shape()] * 2, ((0, None), (1, None)), kvs, slots)
    via_a, via_b = shift(o2a, "zh", 1), shift(o2b, "zh", -1)
    four = ((0, 0), (0, 1), (1, 0), (1, 1))
    o1, o3 = attend([q1, q3], four, [chunk_shape()] * 2, four, kvs, slots)
    m1, m3 = call(pass_kernel, [chunk_shape()] * 2, [VMEM] * 4, o1, o3, via_a, via_b)
    m1, m3, q0 = lax.optimization_barrier((m1, m3, q0))
    back1, back3 = shift(m1, "zh", -1), shift(m3, "zh", 1)
    (o0,) = attend([q0], four[:2], [chunk_shape()], four[:2], kvs, slots)
    whole = call(final_kernel, jax.ShapeDtypeStruct((NU * TOK, HD), BF), [VMEM] * 3, o0, back1, back3)
    home = lax.all_to_all(whole.reshape(NU, TOK, HD), ("y", "zl"), split_axis=0, concat_axis=0, tiled=True)
    return call(unpack_kernel, jax.ShapeDtypeStruct((TOK, HEADS * HD), BF), [VMEM], home)


def solution(mesh):
    fine = Mesh(mesh.devices.reshape(NX, NZ, NC, NU // 2, 2), AXES)
    tokens = P(AXES, None)
    placed = (tokens, tokens, tokens, P(None, AXES[:3], None))
    return jax.shard_map(shards, mesh=fine, in_specs=placed, out_specs=tokens, check_vma=False)
```

```python
import functools
import math

import jax
import jax.numpy as jnp
from jax import lax
from jax.experimental import pallas as pl
from jax.experimental.pallas import tpu as pltpu
from jax.sharding import Mesh, PartitionSpec as P

BF = jnp.bfloat16
F32 = jnp.float32
NX, NZ, NC, NU = 4, 4, 2, 16
HEADS, HD, BS, TOK = 12, 128, 128, 64
SEGB = 8
ROWS = SEGB * BS
PICKS = 16
LSE = 32
STEPS = 4
EXP2 = math.log2(math.e) / math.sqrt(HD)
AXES = ("x", "zh", "core", "y", "zl")
VMEM = pl.BlockSpec(memory_space=pltpu.VMEM)
HBM = pl.BlockSpec(memory_space=pltpu.HBM)


def shift(field, axis, by):
    n = lax.axis_size(axis)
    return lax.ppermute(field, axis, [(i, (i + by) % n) for i in range(n)])


def pack_kernel(q_hbm, k_hbm, v_hbm, mask_hbm, out_ref, picks_ref, q_ref, k_ref, v_ref, mask_ref, sems):
    head = jnp.minimum(lax.axis_index("y") * 2 + lax.axis_index("zl"), HEADS - 1)
    pairs = ((q_hbm, q_ref), (k_hbm, k_ref), (v_hbm, v_ref), (mask_hbm.at[head], mask_ref))
    copies = [pltpu.make_async_copy(src, dst, sems.at[i]) for i, (src, dst) in enumerate(pairs)]
    for copy in copies:
        copy.start()
    for s in range(HEADS, NU):
        out_ref[s] = jnp.zeros((3 * TOK, HD), BF)
    for n, ref in enumerate((q_ref, k_ref, v_ref)):
        copies[n].wait()
        for h in range(HEADS):
            out_ref[h, n * TOK : (n + 1) * TOK, :] = ref[:, h * HD : (h + 1) * HD]
    copies[3].wait()
    live = mask_ref[...].astype(F32).astype(BF)
    cols = live.shape[1]
    i = lax.broadcasted_iota(jnp.int32, (cols, HD), 0)
    g = lax.broadcasted_iota(jnp.int32, (cols, HD), 1)
    weight = jnp.where(i // SEGB == g, i % SEGB, 0).astype(F32).astype(BF)
    picks = jnp.dot(live, weight, preferred_element_type=F32)
    picks_ref[...] = jnp.concatenate([picks, jnp.zeros((PICKS - SEGB, HD), F32)], axis=0).astype(BF)


def split3(lse):
    hi = lse.astype(BF).astype(F32)
    mid = (lse - hi).astype(BF).astype(F32)
    return jnp.concatenate([hi, mid, lse - hi - mid, jnp.zeros_like(hi)], axis=0).astype(BF)


def join3(rows):
    rows = rows.astype(F32)
    return rows[0:SEGB] + rows[SEGB : 2 * SEGB] + rows[2 * SEGB : 3 * SEGB]


def attend_kernel(chunks, shifts, opening, *refs):
    q_refs, (near_ref, far_ref), rest = refs[:chunks], refs[chunks : chunks + 2], refs[chunks + 2 :]
    acc_refs, ml_refs, rest = rest[:chunks], rest[chunks : 2 * chunks], rest[2 * chunks :]
    out_refs = rest[:-3]
    flat_ref, picks_ref, sem = rest[-3:]
    for n, q_ref in enumerate(q_refs):
        flat_ref[n * SEGB : (n + 1) * SEGB, :] = q_ref[ROWS:, :].astype(F32)[:SEGB].astype(jnp.int32)
    fetch = pltpu.make_async_copy(flat_ref, picks_ref, sem)
    fetch.start()
    x, z, c = lax.axis_index("x"), lax.axis_index("zh"), lax.axis_index("core")
    columns = [(x * NZ + (z + NZ - dz) % NZ) * NC + cc for dz in shifts for cc in (c, 1 - c)]
    groups = [ref.at[n] for n in range(len(shifts)) for ref in (near_ref, far_ref)]
    lane = lax.broadcasted_iota(jnp.int32, (BS // STEPS, HD), 1)
    fetch.wait()
    blocks = [(n, b) for n in range(chunks) for b in range(SEGB)]
    fetched, scores, weights, peaks, totals, fades = {}, {}, {}, {}, {}, {}
    lses = [[] for _ in q_refs]
    for t in range(len(blocks) + 2):
        ahead, here, last = t, t - 1, t - 2
        runs = [0 <= i < len(blocks) for i in (ahead, here, last)]
        if runs[0]:
            n, b = blocks[ahead]
            keys, values = [], []
            for group, column in zip(groups, columns):
                both = group[pl.ds(2 * picks_ref[n * SEGB + b, column], 2)]
                keys.append(both[:, :TOK, :].reshape(BS, HD))
                values.append(both[:, TOK:, :].reshape(BS, HD))
            fetched[ahead] = q_refs[n][b * BS : (b + 1) * BS, :], keys, values
            scores[ahead] = []
        if runs[1]:
            weights[here], peaks[here], totals[here], fades[here] = [], [], [], []
        products = []
        for step in range(STEPS):
            pair = slice(2 * step, 2 * step + 2)
            if runs[0] and step < len(shifts):
                q, keys, _ = fetched[ahead]
                both = jnp.concatenate(keys[pair], axis=0)
                scores[ahead].append(
                    lax.dot_general(q, both, (((1,), (1,)), ((), ())), preferred_element_type=F32)
                )
            if runs[1]:
                n, b = blocks[here]
                rows = slice(step * BS // STEPS, (step + 1) * BS // STEPS)
                part = [s[rows] for s in scores[here]]
                peak = jnp.max(functools.reduce(jnp.maximum, part), axis=1, keepdims=True)
                if not opening:
                    old = ml_refs[n][b * BS + rows.start : b * BS + rows.stop, :]
                    old_peak = old[:, 0:1]
                    old_total = jnp.sum(jnp.where(lane == 1, old, 0.0), axis=1, keepdims=True)
                    peak = jnp.maximum(peak, old_peak)
                    fade = jnp.exp2((old_peak - peak) * EXP2)
                    fades[here].append(fade)
                w = [jnp.exp2((s - peak) * EXP2) for s in part]
                total = jnp.sum(functools.reduce(jnp.add, w), axis=1, keepdims=True)
                totals[here].append(total if opening else total + old_total * fade)
                peaks[here].append(peak)
                weights[here].append([p.astype(BF) for p in w])
            if runs[2] and step < len(shifts):
                w = jnp.concatenate([p[step] for p in weights[last]], axis=0)
                both = jnp.concatenate(fetched[last][2][pair], axis=0)
                products.append(jnp.dot(w, both, preferred_element_type=F32))
        if runs[2]:
            n, b = blocks[last]
            rows = slice(b * BS, (b + 1) * BS)
            peak, total = jnp.concatenate(peaks[last], axis=0), jnp.concatenate(totals[last], axis=0)
            if opening:
                acc_refs[n][rows, :] = functools.reduce(jnp.add, products)
                lanes = lax.broadcasted_iota(jnp.int32, (BS, HD), 1)
                ml_refs[n][rows, :] = jnp.where(lanes == 0, peak, total)
            else:
                products.append(acc_refs[n][rows, :] * jnp.concatenate(fades[last], axis=0))
                out_refs[n][rows, :] = (functools.reduce(jnp.add, products) * (1.0 / total)).astype(BF)
                lse = peak * EXP2 + jnp.log2(total)
                lses[n].append(jnp.transpose(jnp.broadcast_to(lse, (BS, HD)))[0:1, :])
                if b == SEGB - 1:
                    out_refs[n][ROWS:, :] = split3(jnp.concatenate(lses[n], axis=0))
            fetched[last] = scores[last] = weights[last] = None


def merge_kernel(*refs):
    ins, out_ref = refs[:-1], refs[-1]
    lses = [join3(r[ROWS:, :]) for r in ins]
    top = functools.reduce(jnp.maximum, lses)
    parts = [jnp.exp2(s - top) for s in lses]
    total = functools.reduce(jnp.add, parts)
    parts = [p / total for p in parts]
    for b in range(SEGB):
        rows = slice(b * BS, (b + 1) * BS)
        acc = jnp.zeros((BS, HD), F32)
        for r, p in zip(ins, parts):
            acc = acc + jnp.transpose(jnp.broadcast_to(p[b : b + 1, :], (BS, HD))) * r[rows, :].astype(F32)
        out_ref[rows, :] = acc.astype(BF)


def unpack_kernel(in_ref, out_ref):
    for h in range(HEADS):
        out_ref[:, h * HD : (h + 1) * HD] = in_ref[h]


def call(kernel, outs, specs, *args, scratch=(), flops=0, moved=1 << 18, vmem=24):
    return pl.pallas_call(
        kernel,
        out_shape=outs,
        in_specs=specs,
        out_specs=jax.tree.map(lambda _: VMEM, outs),
        scratch_shapes=list(scratch),
        compiler_params=pltpu.CompilerParams(vmem_limit_bytes=vmem << 20),
        cost_estimate=pl.CostEstimate(flops=flops, bytes_accessed=moved, transcendentals=0),
    )(*args)


def attend(queries, shifts, near, far, state=None):
    n = len(queries)
    if state is None:
        outs = [jax.ShapeDtypeStruct((ROWS, HD), F32)] * (2 * n)
    else:
        outs = [jax.ShapeDtypeStruct((ROWS + LSE, HD), BF)] * n
    ins = [*queries, near, far, *(state or [])]
    return call(
        functools.partial(attend_kernel, n, shifts, state is None),
        outs, [VMEM] * len(ins), *ins,
        scratch=[pltpu.VMEM((n * SEGB, HD), jnp.int32), pltpu.SMEM((n * SEGB, HD), jnp.int32), pltpu.SemaphoreType.DMA],
        flops=n * len(shifts) * (1 << 27), moved=2 << 20,
    )


def shards(queries, keys, values, block_mask):
    packed, picks = call(
        pack_kernel,
        (jax.ShapeDtypeStruct((NU, 3 * TOK, HD), BF), jax.ShapeDtypeStruct((PICKS, HD), BF)),
        [HBM] * 4, queries, keys, values, block_mask,
        scratch=[pltpu.VMEM(queries.shape, BF)] * 3
        + [pltpu.VMEM(block_mask.shape[1:], jnp.int32), pltpu.SemaphoreType.DMA((4,))],
        vmem=60,
    )
    got = lax.all_to_all(packed, ("y", "zl"), split_axis=0, concat_axis=0, tiled=True)
    k0 = got[:, TOK:]
    q0 = jnp.concatenate([got[:, :TOK].reshape(ROWS, HD), picks], axis=0)

    k1, k3 = shift(k0, "zh", 1), shift(k0, "zh", -1)
    q1, q2, q3 = (shift(q0, "x", dx) for dx in (1, 2, 3))
    k1, k3, q1, q2, q3 = lax.optimization_barrier((k1, k3, q1, q2, q3))
    k2a, k2b = shift(k1[: NU // 2], "zh", 1), shift(k3[NU // 2 :], "zh", -1)
    near = jnp.stack([k0, k1, k3])
    far = shift(near, "core", 1)
    state = attend([q0, q1, q2, q3], (0, 1, 3), near, far)
    k2a, k2b, *state = lax.optimization_barrier((k2a, k2b, *state))
    acc, ml = state[:NX], state[NX:]

    near = jnp.concatenate([k2a, k2b], axis=0)[None]
    far = shift(near, "core", 1)
    (o2,) = attend([q2], (2,), near, far, [acc[2], ml[2]])
    o2, far = lax.optimization_barrier((o2, far))
    back2 = shift(o2, "x", -2)
    o1, o3 = attend([q1, q3], (2,), near, far, [acc[1], acc[3], ml[1], ml[3]])
    o1, o3, far = lax.optimization_barrier((o1, o3, far))
    back1, back3 = shift(o1, "x", -1), shift(o3, "x", -3)
    (o0,) = attend([q0], (2,), near, far, [acc[0], ml[0]])
    whole = call(merge_kernel, jax.ShapeDtypeStruct((ROWS, HD), BF), [VMEM] * NX, o0, back1, back2, back3)
    home = lax.all_to_all(whole.reshape(NU, TOK, HD), ("y", "zl"), split_axis=0, concat_axis=0, tiled=True)
    return call(unpack_kernel, jax.ShapeDtypeStruct((TOK, HEADS * HD), BF), [VMEM], home)


def solution(mesh):
    fine = Mesh(mesh.devices.reshape(NX, NZ, NC, NU // 2, 2), AXES)
    tokens = P(AXES, None)
    placed = (tokens, tokens, tokens, P(None, AXES[:3], None))
    return jax.shard_map(shards, mesh=fine, in_specs=placed, out_specs=tokens, check_vma=False)
```

```python
import functools
import math

import jax
import jax.numpy as jnp
from jax import lax
from jax.experimental import pallas as pl
from jax.experimental.pallas import tpu as pltpu
from jax.sharding import Mesh, PartitionSpec as P

BF = jnp.bfloat16
F32 = jnp.float32
NX, NZ, NC, NU = 4, 4, 2, 16
HEADS, HD, BS, TOK = 12, 128, 128, 64
SEGB = 8
ROWS = SEGB * BS
PICKS = 16
LSE = 32
STEPS = 4
EXP2 = math.log2(math.e) / math.sqrt(HD)
AXES = ("x", "zh", "core", "y", "zl")
VMEM = pl.BlockSpec(memory_space=pltpu.VMEM)
HBM = pl.BlockSpec(memory_space=pltpu.HBM)


def shift(field, axis, by):
    n = lax.axis_size(axis)
    return lax.ppermute(field, axis, [(i, (i + by) % n) for i in range(n)])


def exchange(field, axes):
    return lax.all_to_all(field, axes, split_axis=0, concat_axis=0, tiled=True)


def pack_kernel(q_hbm, k_hbm, v_hbm, mask_hbm, out_ref, picks_ref, q_ref, k_ref, v_ref, mask_ref, sems):
    head = jnp.minimum(lax.axis_index("y") * 2 + lax.axis_index("zl"), HEADS - 1)
    pairs = ((q_hbm, q_ref), (k_hbm, k_ref), (v_hbm, v_ref), (mask_hbm.at[head], mask_ref))
    copies = [pltpu.make_async_copy(src, dst, sems.at[i]) for i, (src, dst) in enumerate(pairs)]
    for copy in copies:
        copy.start()
    for s in range(HEADS, NU):
        out_ref[s] = jnp.zeros((3 * TOK, HD), BF)
    for n, ref in enumerate((q_ref, k_ref, v_ref)):
        copies[n].wait()
        for h in range(HEADS):
            out_ref[h, n * TOK : (n + 1) * TOK, :] = ref[:, h * HD : (h + 1) * HD]
    copies[3].wait()
    live = mask_ref[...].astype(F32).astype(BF)
    cols = live.shape[1]
    i = lax.broadcasted_iota(jnp.int32, (cols, HD), 0)
    g = lax.broadcasted_iota(jnp.int32, (cols, HD), 1)
    weight = jnp.where(i // SEGB == g, i % SEGB, 0).astype(F32).astype(BF)
    picks = jnp.dot(live, weight, preferred_element_type=F32)
    picks_ref[...] = jnp.concatenate([picks, jnp.zeros((PICKS - SEGB, HD), F32)], axis=0).astype(BF)


def split3(lse):
    hi = lse.astype(BF).astype(F32)
    mid = (lse - hi).astype(BF).astype(F32)
    return jnp.concatenate([hi, mid, lse - hi - mid, jnp.zeros_like(hi)], axis=0).astype(BF)


def join3(rows):
    rows = rows.astype(F32)
    return rows[0:SEGB] + rows[SEGB : 2 * SEGB] + rows[2 * SEGB : 3 * SEGB]


def attend_kernel(chunks, shifts, unit, opening, *refs):
    q_refs, (near_ref, far_ref), rest = refs[:chunks], refs[chunks : chunks + 2], refs[chunks + 2 :]
    old_refs = () if opening else rest[:chunks]
    rest = rest[len(old_refs) :]
    out_refs, (flat_ref, picks_ref, sem) = rest[:-3], rest[-3:]
    for n, q_ref in enumerate(q_refs):
        flat_ref[n * SEGB : (n + 1) * SEGB, :] = q_ref[ROWS:, :].astype(F32)[:SEGB].astype(jnp.int32)
    fetch = pltpu.make_async_copy(flat_ref, picks_ref, sem)
    fetch.start()
    x, z, c = lax.axis_index("x"), lax.axis_index("zh"), lax.axis_index("core")
    if not opening:
        out_refs = [out_refs[0].at[(x + NX - n) % NX] for n in range(chunks)]
    columns = [(x * NZ + (z + NZ - dz) % NZ) * NC + cc for dz in shifts for cc in (c, 1 - c)]
    groups = [ref.at[n] for n in range(len(shifts)) for ref in (near_ref, far_ref)]
    fetch.wait()
    blocks = [(n, b) for n in range(chunks) for b in range(SEGB)]
    units = [blocks[i : i + unit] for i in range(0, len(blocks), unit)]
    fetched, scores, weights, peaks, totals, products = {}, {}, {}, {}, {}, {}
    lses = [[] for _ in q_refs]
    for t in range(len(units) + 2):
        ahead, here, last = (units[i] if 0 <= i < len(units) else [] for i in (t, t - 1, t - 2))
        for n, b in ahead:
            keys, values = [], []
            for group, column in zip(groups, columns):
                both = group[pl.ds(2 * picks_ref[n * SEGB + b, column], 2)]
                keys.append(both[:, :TOK, :].reshape(BS, HD))
                values.append(both[:, TOK:, :].reshape(BS, HD))
            fetched[n, b] = q_refs[n][b * BS : (b + 1) * BS, :], keys, values
            scores[n, b] = []
        for block in here:
            weights[block], peaks[block], totals[block] = [], [], []
        for block in last:
            products[block] = []
        for step in range(STEPS):
            pair = slice(2 * step, 2 * step + 2)
            rows = slice(step * BS // STEPS, (step + 1) * BS // STEPS)
            for i in range(unit):
                if i < len(ahead) and step < len(shifts):
                    q, keys, _ = fetched[ahead[i]]
                    both = jnp.concatenate(keys[pair], axis=0)
                    scores[ahead[i]].append(
                        lax.dot_general(q, both, (((1,), (1,)), ((), ())), preferred_element_type=F32)
                    )
                if i < len(here):
                    part = [s[rows] for s in scores[here[i]]]
                    peak = jnp.max(functools.reduce(jnp.maximum, part), axis=1, keepdims=True)
                    w = [jnp.exp2((s - peak) * EXP2) for s in part]
                    totals[here[i]].append(jnp.sum(functools.reduce(jnp.add, w), axis=1, keepdims=True))
                    peaks[here[i]].append(peak)
                    weights[here[i]].append([p.astype(BF) for p in w])
                if i < len(last) and step < len(shifts):
                    w = jnp.concatenate([p[step] for p in weights[last[i]]], axis=0)
                    both = jnp.concatenate(fetched[last[i]][2][pair], axis=0)
                    products[last[i]].append(jnp.dot(w, both, preferred_element_type=F32))
        for block in last:
            n, b = block
            peak, total = jnp.concatenate(peaks[block], axis=0), jnp.concatenate(totals[block], axis=0)
            rows = slice(b * BS, (b + 1) * BS)
            o = functools.reduce(jnp.add, products[block]) * (1.0 / total)
            lse = jnp.broadcast_to(peak * EXP2 + jnp.log2(total), (BS, HD))
            if opening:
                out_refs[n][0, rows, :] = o
                out_refs[n][1, rows, :] = lse
            else:
                old, old_lse = old_refs[n][0, rows, :], old_refs[n][1, rows, :]
                top = jnp.maximum(lse, old_lse)
                share, old_share = jnp.exp2(lse - top), jnp.exp2(old_lse - top)
                total = share + old_share
                out_refs[n][rows, :] = ((o * share + old * old_share) * (1.0 / total)).astype(BF)
                lses[n].append(jnp.transpose(top + jnp.log2(total))[0:1, :])
                if b == SEGB - 1:
                    out_refs[n][ROWS:, :] = split3(jnp.concatenate(lses[n], axis=0))
            fetched[block] = scores[block] = weights[block] = products[block] = None


def merge_kernel(in_ref, out_ref):
    ins = [in_ref.at[n] for n in range(NX)]
    lses = [join3(r[ROWS:, :]) for r in ins]
    top = functools.reduce(jnp.maximum, lses)
    parts = [jnp.exp2(s - top) for s in lses]
    total = functools.reduce(jnp.add, parts)
    parts = [p / total for p in parts]
    for b in range(SEGB):
        rows = slice(b * BS, (b + 1) * BS)
        acc = jnp.zeros((BS, HD), F32)
        for r, p in zip(ins, parts):
            acc = acc + jnp.transpose(jnp.broadcast_to(p[b : b + 1, :], (BS, HD))) * r[rows, :].astype(F32)
        out_ref[rows, :] = acc.astype(BF)


def unpack_kernel(in_ref, out_ref):
    for h in range(HEADS):
        out_ref[:, h * HD : (h + 1) * HD] = in_ref[h]


def call(kernel, outs, specs, *args, scratch=(), flops=0, moved=1 << 18, vmem=24):
    return pl.pallas_call(
        kernel,
        out_shape=outs,
        in_specs=specs,
        out_specs=jax.tree.map(lambda _: VMEM, outs),
        scratch_shapes=list(scratch),
        compiler_params=pltpu.CompilerParams(vmem_limit_bytes=vmem << 20),
        cost_estimate=pl.CostEstimate(flops=flops, bytes_accessed=moved, transcendentals=0),
    )(*args)


def attend(queries, shifts, near, far, old=None):
    n = len(queries)
    if old is None:
        outs = [jax.ShapeDtypeStruct((2, ROWS, HD), F32)] * n
        unit = 4
    else:
        outs = jax.ShapeDtypeStruct((n, ROWS + LSE, HD), BF)
        unit = 8
    ins = [*queries, near, far, *(old or [])]
    return call(
        functools.partial(attend_kernel, n, shifts, unit, old is None),
        outs, [VMEM] * len(ins), *ins,
        scratch=[pltpu.VMEM((n * SEGB, HD), jnp.int32), pltpu.SMEM((n * SEGB, HD), jnp.int32), pltpu.SemaphoreType.DMA],
        flops=n * len(shifts) * (1 << 27), moved=2 << 20,
    )


def shards(queries, keys, values, block_mask):
    packed, picks = call(
        pack_kernel,
        (jax.ShapeDtypeStruct((NU, 3 * TOK, HD), BF), jax.ShapeDtypeStruct((PICKS, HD), BF)),
        [HBM] * 4, queries, keys, values, block_mask,
        scratch=[pltpu.VMEM(queries.shape, BF)] * 3
        + [pltpu.VMEM(block_mask.shape[1:], jnp.int32), pltpu.SemaphoreType.DMA((4,))],
        vmem=60,
    )
    got = exchange(packed, ("y", "zl"))
    k0 = got[:, TOK:]
    q0 = jnp.concatenate([got[:, :TOK].reshape(ROWS, HD), picks], axis=0)

    k1, k3 = shift(k0, "zh", 1), shift(k0, "zh", -1)
    q1, q2, q3 = (shift(q0, "x", dx) for dx in (1, 2, 3))
    k1, k3, q1, q2, q3 = lax.optimization_barrier((k1, k3, q1, q2, q3))
    k2a, k2b = shift(k1[: NU // 2], "zh", 1), shift(k3[NU // 2 :], "zh", -1)
    near = jnp.stack([k0, k1, k3])
    far = shift(near, "core", 1)
    old = attend([q0, q1, q2, q3], (0, 1, 3), near, far)

    k2a, k2b, *old = lax.optimization_barrier((k2a, k2b, *old))
    near = jnp.concatenate([k2a, k2b], axis=0)[None]
    far = shift(near, "core", 1)
    parts = attend([q0, q1, q2, q3], (2,), near, far, old)
    parts = exchange(parts, "x")
    whole = call(merge_kernel, jax.ShapeDtypeStruct((ROWS, HD), BF), [VMEM], parts)
    home = exchange(whole.reshape(NU, TOK, HD), ("y", "zl"))
    return call(unpack_kernel, jax.ShapeDtypeStruct((TOK, HEADS * HD), BF), [VMEM], home)


def solution(mesh):
    fine = Mesh(mesh.devices.reshape(NX, NZ, NC, NU // 2, 2), AXES)
    tokens = P(AXES, None)
    placed = (tokens, tokens, tokens, P(None, AXES[:3], None))
    return jax.shard_map(shards, mesh=fine, in_specs=placed, out_specs=tokens, check_vma=False)
```

```python
import functools
import math

import jax
import jax.numpy as jnp
from jax import lax
from jax.experimental import pallas as pl
from jax.experimental.pallas import tpu as pltpu
from jax.sharding import Mesh, PartitionSpec as P

BF = jnp.bfloat16
F32 = jnp.float32
NX, NZ, NC, NU = 4, 4, 2, 16
HEADS, HD, BS, TOK = 12, 128, 128, 64
SEGB = 8
GROUPS = NX * NC
HALF = 4
ROWS = HALF * BS
EXTRA = 16
EXP2 = math.log2(math.e) / math.sqrt(HD)
UNIT = 2
SHIFTS = (0, 1, 3, 2)
AXES = ("x", "zh", "core", "y", "zl")
VMEM = pl.BlockSpec(memory_space=pltpu.VMEM)
HBM = pl.BlockSpec(memory_space=pltpu.HBM)


def shift(field, axis, by):
    n = lax.axis_size(axis)
    return lax.ppermute(field, axis, [(i, (i + by) % n) for i in range(n)])


def pack_kernel(q_hbm, k_hbm, v_hbm, mask_hbm, out_ref, picks_ref, q_ref, k_ref, v_ref, mask_ref, sems):
    head = jnp.minimum(lax.axis_index("y") * 2 + lax.axis_index("zl"), HEADS - 1)
    pairs = ((q_hbm, q_ref), (k_hbm, k_ref), (v_hbm, v_ref), (mask_hbm.at[head], mask_ref))
    copies = [pltpu.make_async_copy(src, dst, sems.at[i]) for i, (src, dst) in enumerate(pairs)]
    for copy in copies:
        copy.start()
    for s in range(HEADS, NU):
        out_ref[s] = jnp.zeros((3 * TOK, HD), BF)
    for n, ref in enumerate((q_ref, k_ref, v_ref)):
        copies[n].wait()
        for h in range(HEADS):
            out_ref[h, n * TOK : (n + 1) * TOK, :] = ref[:, h * HD : (h + 1) * HD]
    copies[3].wait()
    live = mask_ref[...].astype(F32).astype(BF)
    cols = live.shape[1]
    i = lax.broadcasted_iota(jnp.int32, (cols, HD), 0)
    g = lax.broadcasted_iota(jnp.int32, (cols, HD), 1)
    weight = jnp.where(i // SEGB == g, i % SEGB, 0).astype(F32).astype(BF)
    picks = jnp.dot(live, weight, preferred_element_type=F32)
    pad = jnp.zeros((EXTRA - HALF, HD), F32)
    for half in range(2):
        picks_ref[half] = jnp.concatenate([picks[half * HALF : (half + 1) * HALF], pad], axis=0).astype(BF)


def split3(lse):
    hi = lse.astype(BF).astype(F32)
    mid = (lse - hi).astype(BF).astype(F32)
    return jnp.concatenate([hi, mid, lse - hi - mid, jnp.zeros_like(hi)], axis=0).astype(BF)


def join3(rows):
    rows = rows.astype(F32)
    return rows[0:HALF] + rows[HALF : 2 * HALF] + rows[2 * HALF : 3 * HALF]


def attend_kernel(halves, n_q, kv_slots, out_slots, *refs):
    def view(group, slot):
        return group[slot[0]] if slot[1] is None else group[slot[0]].at[slot[1]]

    n_kv, n_out = max(r for r, _ in kv_slots) + 1, max(r for r, _ in out_slots) + 1
    q_refs, kv_refs, out_refs = refs[:n_q], refs[n_q : n_q + n_kv], refs[n_q + n_kv : n_q + n_kv + n_out]
    flat_ref, picks_ref, sem = refs[n_q + n_kv + n_out :]
    for h, slot in enumerate(halves):
        flat_ref[h * SEGB : (h + 1) * SEGB, :] = view(q_refs, slot)[ROWS:, :].astype(F32)[:SEGB].astype(jnp.int32)
    fetch = pltpu.make_async_copy(flat_ref, picks_ref, sem)
    fetch.start()
    x, z, c = lax.axis_index("x"), lax.axis_index("zh"), lax.axis_index("core")
    columns = [((x + NX - dx) % NX * NZ + z) * NC + cc for dx in SHIFTS for cc in (c, 1 - c)]
    groups = [view(kv_refs, slot) for slot in kv_slots]
    outs = [view(out_refs, slot) for slot in out_slots]
    fetch.wait()
    blocks = [(h, b) for h in range(len(halves)) for b in range(HALF)]
    units = [blocks[i : i + UNIT] for i in range(0, len(blocks), UNIT)]
    fetched, scores, weights, peaks, totals, products = {}, {}, {}, {}, {}, {}
    lses = [[] for _ in halves]
    for t in range(len(units) + 2):
        ahead, here, last = (units[i] if 0 <= i < len(units) else [] for i in (t, t - 1, t - 2))
        for h, b in ahead:
            keys, values = [], []
            for group, column in zip(groups, columns):
                both = group[pl.ds(2 * picks_ref[h * SEGB + b, column], 2)]
                keys.append(both[:, :TOK, :].reshape(BS, HD))
                values.append(both[:, TOK:, :].reshape(BS, HD))
            fetched[h, b] = view(q_refs, halves[h])[b * BS : (b + 1) * BS, :], keys, values
            scores[h, b] = []
        for block in here:
            weights[block], peaks[block], totals[block] = [], [], []
        for block in last:
            products[block] = []
        for step in range(4):
            pair = slice(2 * step, 2 * step + 2)
            rows = slice(step * BS // 4, (step + 1) * BS // 4)
            for i in range(UNIT):
                if i < len(ahead):
                    q, keys, _ = fetched[ahead[i]]
                    both = jnp.concatenate(keys[pair], axis=0)
                    scores[ahead[i]].append(
                        lax.dot_general(q, both, (((1,), (1,)), ((), ())), preferred_element_type=F32)
                    )
                if i < len(here):
                    part = [s[rows] for s in scores[here[i]]]
                    peak = jnp.max(functools.reduce(jnp.maximum, part), axis=1, keepdims=True)
                    w = [jnp.exp2((s - peak) * EXP2) for s in part]
                    totals[here[i]].append(jnp.sum(functools.reduce(jnp.add, w), axis=1, keepdims=True))
                    peaks[here[i]].append(peak)
                    weights[here[i]].append([p.astype(BF) for p in w])
                if i < len(last):
                    w = jnp.concatenate([p[step] for p in weights[last[i]]], axis=0)
                    both = jnp.concatenate(fetched[last[i]][2][pair], axis=0)
                    products[last[i]].append(jnp.dot(w, both, preferred_element_type=F32))
        for block in last:
            h, b = block
            peak, total = jnp.concatenate(peaks[block], axis=0), jnp.concatenate(totals[block], axis=0)
            o = functools.reduce(jnp.add, products[block]) * (1.0 / total)
            outs[h][b * BS : (b + 1) * BS, :] = o.astype(BF)
            lse = peak * EXP2 + jnp.log2(total)
            lses[h].append(jnp.transpose(jnp.broadcast_to(lse, (BS, HD)))[0:1, :])
            if b == HALF - 1:
                outs[h][ROWS:, :] = split3(jnp.concatenate(lses[h], axis=0))
            fetched[block] = scores[block] = weights[block] = products[block] = None


def merge_halves(ins, out_ref, first, keep):
    lses = [join3(r[ROWS:, :]) for r in ins]
    top = functools.reduce(jnp.maximum, lses)
    parts = [jnp.exp2(s - top) for s in lses]
    total = functools.reduce(jnp.add, parts)
    parts = [p / total for p in parts]
    for b in range(HALF):
        rows = slice(b * BS, (b + 1) * BS)
        acc = jnp.zeros((BS, HD), F32)
        for r, p in zip(ins, parts):
            acc = acc + jnp.transpose(jnp.broadcast_to(p[b : b + 1, :], (BS, HD))) * r[rows, :].astype(F32)
        out_ref[first + b * BS : first + (b + 1) * BS, :] = acc.astype(BF)
    if keep:
        out_ref[ROWS:, :] = split3(top + jnp.log2(total))


def pass_kernel(o1_ref, o3_ref, via_a_ref, via_b_ref, out1_ref, out3_ref):
    out1_ref[0] = o1_ref[0]
    merge_halves([o1_ref.at[1], via_b_ref], out1_ref.at[1], 0, True)
    merge_halves([o3_ref.at[0], via_a_ref], out3_ref.at[0], 0, True)
    out3_ref[1] = o3_ref[1]


def final_kernel(a_ref, b_ref, c_ref, out_ref):
    for half in range(2):
        merge_halves([r.at[half] for r in (a_ref, b_ref, c_ref)], out_ref, half * ROWS, False)


def unpack_kernel(in_ref, out_ref):
    for h in range(HEADS):
        out_ref[:, h * HD : (h + 1) * HD] = in_ref[h]


def call(kernel, outs, specs, *args, scratch=(), flops=0, moved=1 << 18, vmem=24):
    return pl.pallas_call(
        kernel,
        out_shape=outs,
        in_specs=specs,
        out_specs=jax.tree.map(lambda _: VMEM, outs),
        scratch_shapes=list(scratch),
        compiler_params=pltpu.CompilerParams(vmem_limit_bytes=vmem << 20),
        cost_estimate=pl.CostEstimate(flops=flops, bytes_accessed=moved, transcendentals=0),
    )(*args)


def half_shape():
    return jax.ShapeDtypeStruct((ROWS + EXTRA, HD), BF)


def chunk_shape():
    return jax.ShapeDtypeStruct((2, ROWS + EXTRA, HD), BF)


def attend(queries, halves, outs, out_slots, kvs, kv_slots):
    n = len(halves)
    return call(
        functools.partial(attend_kernel, halves, len(queries), kv_slots, out_slots),
        outs, [VMEM] * (len(queries) + len(kvs)), *queries, *kvs,
        scratch=[pltpu.VMEM((n * SEGB, HD), jnp.int32), pltpu.SMEM((n * SEGB, HD), jnp.int32), pltpu.SemaphoreType.DMA],
        flops=n * (1 << 28), moved=4 << 20,
    )


def shards(queries, keys, values, block_mask):
    packed, picks = call(
        pack_kernel,
        (jax.ShapeDtypeStruct((NU, 3 * TOK, HD), BF), jax.ShapeDtypeStruct((2, EXTRA, HD), BF)),
        [HBM] * 4, queries, keys, values, block_mask,
        scratch=[pltpu.VMEM(queries.shape, BF)] * 3
        + [pltpu.VMEM(block_mask.shape[1:], jnp.int32), pltpu.SemaphoreType.DMA((4,))],
        vmem=60,
    )
    got = lax.all_to_all(packed, ("y", "zl"), split_axis=0, concat_axis=0, tiled=True)
    k0 = got[:, TOK:]
    q0 = jnp.concatenate([got[:, :TOK].reshape(2, ROWS, HD), picks], axis=1)

    k1, k3, k2 = (shift(k0, "x", dx) for dx in SHIFTS[1:])
    q1, q3 = shift(q0, "zh", 1), shift(q0, "zh", -1)
    k1, k3, k2, q1, q3 = lax.optimization_barrier((k1, k3, k2, q1, q3))
    near = jnp.stack([k0, k1, k3, k2])
    far = shift(near, "core", 1)
    q2a, q2b = shift(q1[0], "zh", 1), shift(q3[1], "zh", -1)
    kvs = [near, far]
    slots = tuple((ref, n) for n in range(NX) for ref in range(NC))

    four = ((0, 0), (0, 1), (1, 0), (1, 1))
    o1, o3 = attend([q1, q3], four, [chunk_shape()] * 2, four, kvs, slots)
    q2a, q2b, o1, o3 = lax.optimization_barrier((q2a, q2b, o1, o3))
    o2a, o2b = attend([q2a, q2b], ((0, None), (1, None)), [half_shape()] * 2, ((0, None), (1, None)), kvs, slots)
    via_a, via_b = shift(o2a, "zh", 1), shift(o2b, "zh", -1)
    q0, o2a, o2b = lax.optimization_barrier((q0, o2a, o2b))
    (o0,) = attend([q0], four[:2], [chunk_shape()], four[:2], kvs, slots)
    via_a, via_b, o0 = lax.optimization_barrier((via_a, via_b, o0))
    m1, m3 = call(pass_kernel, [chunk_shape()] * 2, [VMEM] * 4, o1, o3, via_a, via_b)
    back1, back3 = shift(m1, "zh", -1), shift(m3, "zh", 1)
    whole = call(final_kernel, jax.ShapeDtypeStruct((NU * TOK, HD), BF), [VMEM] * 3, o0, back1, back3)
    home = lax.all_to_all(whole.reshape(NU, TOK, HD), ("y", "zl"), split_axis=0, concat_axis=0, tiled=True)
    return call(unpack_kernel, jax.ShapeDtypeStruct((TOK, HEADS * HD), BF), [VMEM], home)


def solution(mesh):
    fine = Mesh(mesh.devices.reshape(NX, NZ, NC, NU // 2, 2), AXES)
    tokens = P(AXES, None)
    placed = (tokens, tokens, tokens, P(None, AXES[:3], None))
    return jax.shard_map(shards, mesh=fine, in_specs=placed, out_specs=tokens, check_vma=False)
```

```python
import functools
import math

import jax
import jax.numpy as jnp
from jax import lax
from jax.experimental import pallas as pl
from jax.experimental.pallas import tpu as pltpu
from jax.sharding import Mesh, PartitionSpec as P

BF = jnp.bfloat16
F32 = jnp.float32
NX, NZ, NC, NU = 4, 4, 2, 16
HEADS, HD, BS, TOK = 12, 128, 128, 64
SEGB = 8
ROWS = SEGB * BS
PICKS = 16
LSE = 32
STEPS = 4
EXP2 = math.log2(math.e) / math.sqrt(HD)
AXES = ("x", "zh", "core", "y", "zl")
VMEM = pl.BlockSpec(memory_space=pltpu.VMEM)
HBM = pl.BlockSpec(memory_space=pltpu.HBM)


def shift(field, axis, by):
    n = lax.axis_size(axis)
    return lax.ppermute(field, axis, [(i, (i + by) % n) for i in range(n)])


def exchange(field, axes):
    return lax.all_to_all(field, axes, split_axis=0, concat_axis=0, tiled=True)


def pack_kernel(q_hbm, k_hbm, v_hbm, mask_hbm, out_ref, picks_ref, q_ref, k_ref, v_ref, mask_ref, sems):
    head = jnp.minimum(lax.axis_index("y") * 2 + lax.axis_index("zl"), HEADS - 1)
    pairs = ((q_hbm, q_ref), (k_hbm, k_ref), (v_hbm, v_ref), (mask_hbm.at[head], mask_ref))
    copies = [pltpu.make_async_copy(src, dst, sems.at[i]) for i, (src, dst) in enumerate(pairs)]
    for copy in copies:
        copy.start()
    for s in range(HEADS, NU):
        out_ref[s] = jnp.zeros((3 * TOK, HD), BF)
    for n, ref in enumerate((q_ref, k_ref, v_ref)):
        copies[n].wait()
        for h in range(HEADS):
            out_ref[h, n * TOK : (n + 1) * TOK, :] = ref[:, h * HD : (h + 1) * HD]
    copies[3].wait()
    live = mask_ref[...].astype(F32).astype(BF)
    cols = live.shape[1]
    i = lax.broadcasted_iota(jnp.int32, (cols, HD), 0)
    g = lax.broadcasted_iota(jnp.int32, (cols, HD), 1)
    weight = jnp.where(i // SEGB == g, i % SEGB, 0).astype(F32).astype(BF)
    picks = jnp.dot(live, weight, preferred_element_type=F32)
    picks_ref[...] = jnp.concatenate([picks, jnp.zeros((PICKS - SEGB, HD), F32)], axis=0).astype(BF)


def split3(lse):
    hi = lse.astype(BF).astype(F32)
    mid = (lse - hi).astype(BF).astype(F32)
    return jnp.concatenate([hi, mid, lse - hi - mid, jnp.zeros_like(hi)], axis=0).astype(BF)


def join3(rows):
    rows = rows.astype(F32)
    return rows[0:SEGB] + rows[SEGB : 2 * SEGB] + rows[2 * SEGB : 3 * SEGB]


def attend_kernel(chunks, shifts, unit, opening, *refs):
    q_refs, (near_ref, far_ref), rest = refs[:chunks], refs[chunks : chunks + 2], refs[chunks + 2 :]
    old_refs = () if opening else rest[:chunks]
    rest = rest[len(old_refs) :]
    out_refs, (flat_ref, picks_ref, sem) = rest[:chunks], rest[chunks:]
    for n, q_ref in enumerate(q_refs):
        flat_ref[n * SEGB : (n + 1) * SEGB, :] = q_ref[ROWS:, :].astype(F32)[:SEGB].astype(jnp.int32)
    fetch = pltpu.make_async_copy(flat_ref, picks_ref, sem)
    fetch.start()
    x, z, c = lax.axis_index("x"), lax.axis_index("zh"), lax.axis_index("core")
    columns = [(x * NZ + (z + NZ - dz) % NZ) * NC + cc for dz in shifts for cc in (c, 1 - c)]
    groups = [ref.at[n] for n in range(len(shifts)) for ref in (near_ref, far_ref)]
    fetch.wait()
    blocks = [(n, b) for n in range(chunks) for b in range(SEGB)]
    units = [blocks[i : i + unit] for i in range(0, len(blocks), unit)]
    fetched, scores, weights, peaks, totals, products = {}, {}, {}, {}, {}, {}
    lses = [[] for _ in q_refs]
    for t in range(len(units) + 2):
        ahead, here, last = (units[i] if 0 <= i < len(units) else [] for i in (t, t - 1, t - 2))
        for n, b in ahead:
            keys, values = [], []
            for group, column in zip(groups, columns):
                both = group[pl.ds(2 * picks_ref[n * SEGB + b, column], 2)]
                keys.append(both[:, :TOK, :].reshape(BS, HD))
                values.append(both[:, TOK:, :].reshape(BS, HD))
            fetched[n, b] = q_refs[n][b * BS : (b + 1) * BS, :], keys, values
            scores[n, b] = []
        for block in here:
            weights[block], peaks[block], totals[block] = [], [], []
        for block in last:
            products[block] = []
        for step in range(STEPS):
            pair = slice(2 * step, 2 * step + 2)
            rows = slice(step * BS // STEPS, (step + 1) * BS // STEPS)
            for i in range(unit):
                if i < len(ahead) and step < len(shifts):
                    q, keys, _ = fetched[ahead[i]]
                    both = jnp.concatenate(keys[pair], axis=0)
                    scores[ahead[i]].append(
                        lax.dot_general(q, both, (((1,), (1,)), ((), ())), preferred_element_type=F32)
                    )
                if i < len(here):
                    part = [s[rows] for s in scores[here[i]]]
                    peak = jnp.max(functools.reduce(jnp.maximum, part), axis=1, keepdims=True)
                    w = [jnp.exp2((s - peak) * EXP2) for s in part]
                    totals[here[i]].append(jnp.sum(functools.reduce(jnp.add, w), axis=1, keepdims=True))
                    peaks[here[i]].append(peak)
                    weights[here[i]].append([p.astype(BF) for p in w])
                if i < len(last) and step < len(shifts):
                    w = jnp.concatenate([p[step] for p in weights[last[i]]], axis=0)
                    both = jnp.concatenate(fetched[last[i]][2][pair], axis=0)
                    products[last[i]].append(jnp.dot(w, both, preferred_element_type=F32))
        for block in last:
            n, b = block
            peak, total = jnp.concatenate(peaks[block], axis=0), jnp.concatenate(totals[block], axis=0)
            rows = slice(b * BS, (b + 1) * BS)
            o = functools.reduce(jnp.add, products[block]) * (1.0 / total)
            lse = jnp.broadcast_to(peak * EXP2 + jnp.log2(total), (BS, HD))
            if opening:
                out_refs[n][0, rows, :] = o
                out_refs[n][1, rows, :] = lse
            else:
                old, old_lse = old_refs[n][0, rows, :], old_refs[n][1, rows, :]
                top = jnp.maximum(lse, old_lse)
                share, old_share = jnp.exp2(lse - top), jnp.exp2(old_lse - top)
                total = share + old_share
                out_refs[n][rows, :] = ((o * share + old * old_share) * (1.0 / total)).astype(BF)
                lses[n].append(jnp.transpose(top + jnp.log2(total))[0:1, :])
                if b == SEGB - 1:
                    out_refs[n][ROWS:, :] = split3(jnp.concatenate(lses[n], axis=0))
            fetched[block] = scores[block] = weights[block] = products[block] = None


def merge_kernel(keep, *refs):
    ins, out_ref = refs[:-1], refs[-1]
    lses = [join3(r[ROWS:, :]) for r in ins]
    top = functools.reduce(jnp.maximum, lses)
    parts = [jnp.exp2(s - top) for s in lses]
    total = functools.reduce(jnp.add, parts)
    parts = [p / total for p in parts]
    for b in range(SEGB):
        rows = slice(b * BS, (b + 1) * BS)
        acc = jnp.zeros((BS, HD), F32)
        for r, p in zip(ins, parts):
            acc = acc + jnp.transpose(jnp.broadcast_to(p[b : b + 1, :], (BS, HD))) * r[rows, :].astype(F32)
        out_ref[rows, :] = acc.astype(out_ref.dtype)
    if keep:
        out_ref[ROWS:, :] = split3(top + jnp.log2(total))


def unpack_kernel(in_ref, out_ref):
    for h in range(HEADS):
        out_ref[:, h * HD : (h + 1) * HD] = in_ref[h]


def call(kernel, outs, specs, *args, scratch=(), flops=0, moved=1 << 18, vmem=24):
    return pl.pallas_call(
        kernel,
        out_shape=outs,
        in_specs=specs,
        out_specs=jax.tree.map(lambda _: VMEM, outs),
        scratch_shapes=list(scratch),
        compiler_params=pltpu.CompilerParams(vmem_limit_bytes=vmem << 20),
        cost_estimate=pl.CostEstimate(flops=flops, bytes_accessed=moved, transcendentals=0),
    )(*args)


def attend(queries, shifts, near, far, old=None):
    n = len(queries)
    if old is None:
        outs = [jax.ShapeDtypeStruct((2, ROWS, HD), F32)] * n
        unit = 4
    else:
        outs = [jax.ShapeDtypeStruct((ROWS + LSE, HD), BF)] * n
        unit = 8
    ins = [*queries, near, far, *(old or [])]
    return call(
        functools.partial(attend_kernel, n, shifts, unit, old is None),
        outs, [VMEM] * len(ins), *ins,
        scratch=[pltpu.VMEM((n * SEGB, HD), jnp.int32), pltpu.SMEM((n * SEGB, HD), jnp.int32), pltpu.SemaphoreType.DMA],
        flops=n * len(shifts) * (1 << 27), moved=2 << 20,
    )


def merge(keep, flops, *ins):
    out = jax.ShapeDtypeStruct((ROWS + LSE if keep else ROWS, HD), BF)
    return call(functools.partial(merge_kernel, keep), out, [VMEM] * len(ins), *ins, flops=flops)


def shards(queries, keys, values, block_mask):
    packed, picks = call(
        pack_kernel,
        (jax.ShapeDtypeStruct((NU, 3 * TOK, HD), BF), jax.ShapeDtypeStruct((PICKS, HD), BF)),
        [HBM] * 4, queries, keys, values, block_mask,
        scratch=[pltpu.VMEM(queries.shape, BF)] * 3
        + [pltpu.VMEM(block_mask.shape[1:], jnp.int32), pltpu.SemaphoreType.DMA((4,))],
        vmem=60,
    )
    got = exchange(packed, ("y", "zl"))
    k0 = got[:, TOK:]
    q0 = jnp.concatenate([got[:, :TOK].reshape(ROWS, HD), picks], axis=0)

    k1, k3 = shift(k0, "zh", 1), shift(k0, "zh", -1)
    q1, q2, q3 = (shift(q0, "x", dx) for dx in (1, 2, 3))
    k1, k3, q1, q2, q3 = lax.optimization_barrier((k1, k3, q1, q2, q3))
    k2a, k2b = shift(k1[: NU // 2], "zh", 1), shift(k3[NU // 2 :], "zh", -1)
    near = jnp.stack([k0, k1, k3])
    far = shift(near, "core", 1)
    old = attend([q0, q1, q2, q3], (0, 1, 3), near, far)

    k2a, k2b, *old = lax.optimization_barrier((k2a, k2b, *old))
    near = jnp.concatenate([k2a, k2b], axis=0)[None]
    far = shift(near, "core", 1)
    (o2,) = attend([q2], (2,), near, far, [old[2]])
    o2, far = lax.optimization_barrier((o2, far))
    back2 = shift(o2, "x", -2)
    o1, o3 = attend([q1, q3], (2,), near, far, [old[1], old[3]])
    o1, o3, far = lax.optimization_barrier((o1, o3, far))
    back1, back3 = shift(o1, "x", -1), shift(o3, "x", -3)
    (o0,) = attend([q0], (2,), near, far, [old[0]])
    first = merge(True, 1 << 33, o0, back2)
    whole = merge(False, 0, first, back1, back3)
    home = exchange(whole.reshape(NU, TOK, HD), ("y", "zl"))
    return call(unpack_kernel, jax.ShapeDtypeStruct((TOK, HEADS * HD), BF), [VMEM], home)


def solution(mesh):
    fine = Mesh(mesh.devices.reshape(NX, NZ, NC, NU // 2, 2), AXES)
    tokens = P(AXES, None)
    placed = (tokens, tokens, tokens, P(None, AXES[:3], None))
    return jax.shard_map(shards, mesh=fine, in_specs=placed, out_specs=tokens, check_vma=False)
```

```python
import functools
import math

import jax
import jax.numpy as jnp
from jax import lax
from jax.experimental import pallas as pl
from jax.experimental.pallas import tpu as pltpu
from jax.sharding import Mesh, PartitionSpec as P

BF = jnp.bfloat16
F32 = jnp.float32
NX, NZ, NC, NU = 4, 4, 2, 16
HEADS, HD, BS, TOK = 12, 128, 128, 64
SEGB = 8
ROWS = SEGB * BS
PICKS = 16
LSE = 32
STEPS = 4
EXP2 = math.log2(math.e) / math.sqrt(HD)
AXES = ("x", "zh", "core", "y", "zl")
VMEM = pl.BlockSpec(memory_space=pltpu.VMEM)
HBM = pl.BlockSpec(memory_space=pltpu.HBM)


def shift(field, axis, by):
    n = lax.axis_size(axis)
    return lax.ppermute(field, axis, [(i, (i + by) % n) for i in range(n)])


def ring_step(field):
    pairs = [(z * NC + c, (z + (1, -1)[c]) % NZ * NC + c) for z in range(NZ) for c in range(NC)]
    return lax.ppermute(field, ("zh", "core"), pairs)


def exchange(field, axes):
    return lax.all_to_all(field, axes, split_axis=0, concat_axis=0, tiled=True)


def pack_kernel(q_hbm, k_hbm, v_hbm, mask_hbm, out_ref, picks_ref, q_ref, k_ref, v_ref, mask_ref, sems):
    head = jnp.minimum(lax.axis_index("y") * 2 + lax.axis_index("zl"), HEADS - 1)
    pairs = ((q_hbm, q_ref), (k_hbm, k_ref), (v_hbm, v_ref), (mask_hbm.at[head], mask_ref))
    copies = [pltpu.make_async_copy(src, dst, sems.at[i]) for i, (src, dst) in enumerate(pairs)]
    for copy in copies:
        copy.start()
    for s in range(HEADS, NU):
        out_ref[s] = jnp.zeros((3 * TOK, HD), BF)
    for n, ref in enumerate((q_ref, k_ref, v_ref)):
        copies[n].wait()
        for h in range(HEADS):
            out_ref[h, n * TOK : (n + 1) * TOK, :] = ref[:, h * HD : (h + 1) * HD]
    copies[3].wait()
    live = mask_ref[...].astype(F32).astype(BF)
    cols = live.shape[1]
    i = lax.broadcasted_iota(jnp.int32, (cols, HD), 0)
    g = lax.broadcasted_iota(jnp.int32, (cols, HD), 1)
    weight = jnp.where(i // SEGB == g, i % SEGB, 0).astype(F32).astype(BF)
    picks = jnp.dot(live, weight, preferred_element_type=F32)
    picks_ref[...] = jnp.concatenate([picks, jnp.zeros((PICKS - SEGB, HD), F32)], axis=0).astype(BF)


def split3(lse):
    hi = lse.astype(BF).astype(F32)
    mid = (lse - hi).astype(BF).astype(F32)
    return jnp.concatenate([hi, mid, lse - hi - mid, jnp.zeros_like(hi)], axis=0).astype(BF)


def join3(rows):
    rows = rows.astype(F32)
    return rows[0:SEGB] + rows[SEGB : 2 * SEGB] + rows[2 * SEGB : 3 * SEGB]


def attend_kernel(chunks, unit, opening, *refs):
    n_kv = 3 if opening else 1
    q_refs, kv_refs, rest = refs[:chunks], refs[chunks : chunks + n_kv], refs[chunks + n_kv :]
    old_refs = () if opening else rest[:chunks]
    rest = rest[len(old_refs) :]
    out_refs, (flat_ref, picks_ref, sem) = rest[:chunks], rest[chunks:]
    for n, q_ref in enumerate(q_refs):
        flat_ref[n * SEGB : (n + 1) * SEGB, :] = q_ref[ROWS:, :].astype(F32)[:SEGB].astype(jnp.int32)
    fetch = pltpu.make_async_copy(flat_ref, picks_ref, sem)
    fetch.start()
    x, z, c = lax.axis_index("x"), lax.axis_index("zh"), lax.axis_index("core")
    if opening:
        own, near, far = kv_refs
        before, after = z + NZ - 1 + 2 * c, z + NZ + 1 - 2 * c
        groups = [(own, 0, z, c), (own, 1, z, 1 - c), (near, 0, before, c), (near, 1, before, 1 - c)]
        groups += [(far, 0, after, 1 - c), (far, 1, after, c)]
    else:
        groups = [(kv_refs[0], 0, z + 2, c), (kv_refs[0], 1, z + 2, 1 - c)]
    columns = [(x * NZ + lax.rem(zz, NZ)) * NC + cc for _, _, zz, cc in groups]
    pairs = len(groups) // 2

    def pick(group, j):
        ref, n = group[:2]
        if opening:
            return ref[n, pl.ds(2 * j, 2)]
        return ref[jnp.where(j // (SEGB // 2) == c, n, 3 - n), pl.ds(2 * lax.rem(j, SEGB // 2), 2)]

    fetch.wait()
    blocks = [(n, b) for n in range(chunks) for b in range(SEGB)]
    units = [blocks[i : i + unit] for i in range(0, len(blocks), unit)]
    fetched, scores, weights, peaks, totals, products = {}, {}, {}, {}, {}, {}
    lses = [[] for _ in q_refs]
    for t in range(len(units) + 2):
        ahead, here, last = (units[i] if 0 <= i < len(units) else [] for i in (t, t - 1, t - 2))
        for n, b in ahead:
            keys, values = [], []
            for group, column in zip(groups, columns):
                both = pick(group, picks_ref[n * SEGB + b, column])
                keys.append(both[:, :TOK, :].reshape(BS, HD))
                values.append(both[:, TOK:, :].reshape(BS, HD))
            fetched[n, b] = q_refs[n][b * BS : (b + 1) * BS, :], keys, values
            scores[n, b] = []
        for block in here:
            weights[block], peaks[block], totals[block] = [], [], []
        for block in last:
            products[block] = []
        for step in range(STEPS):
            pair = slice(2 * step, 2 * step + 2)
            rows = slice(step * BS // STEPS, (step + 1) * BS // STEPS)
            for i in range(unit):
                if i < len(ahead) and step < pairs:
                    q, keys, _ = fetched[ahead[i]]
                    both = jnp.concatenate(keys[pair], axis=0)
                    scores[ahead[i]].append(
                        lax.dot_general(q, both, (((1,), (1,)), ((), ())), preferred_element_type=F32)
                    )
                if i < len(here):
                    part = [s[rows] for s in scores[here[i]]]
                    peak = jnp.max(functools.reduce(jnp.maximum, part), axis=1, keepdims=True)
                    w = [jnp.exp2((s - peak) * EXP2) for s in part]
                    totals[here[i]].append(jnp.sum(functools.reduce(jnp.add, w), axis=1, keepdims=True))
                    peaks[here[i]].append(peak)
                    weights[here[i]].append([p.astype(BF) for p in w])
                if i < len(last) and step < pairs:
                    w = jnp.concatenate([p[step] for p in weights[last[i]]], axis=0)
                    both = jnp.concatenate(fetched[last[i]][2][pair], axis=0)
                    products[last[i]].append(jnp.dot(w, both, preferred_element_type=F32))
        for block in last:
            n, b = block
            peak, total = jnp.concatenate(peaks[block], axis=0), jnp.concatenate(totals[block], axis=0)
            rows = slice(b * BS, (b + 1) * BS)
            o = functools.reduce(jnp.add, products[block]) * (1.0 / total)
            lse = jnp.broadcast_to(peak * EXP2 + jnp.log2(total), (BS, HD))
            if opening:
                out_refs[n][0, rows, :] = o
                out_refs[n][1, rows, :] = lse
            else:
                old, old_lse = old_refs[n][0, rows, :], old_refs[n][1, rows, :]
                top = jnp.maximum(lse, old_lse)
                share, old_share = jnp.exp2(lse - top), jnp.exp2(old_lse - top)
                total = share + old_share
                out_refs[n][rows, :] = ((o * share + old * old_share) * (1.0 / total)).astype(BF)
                lses[n].append(jnp.transpose(top + jnp.log2(total))[0:1, :])
                if b == SEGB - 1:
                    out_refs[n][ROWS:, :] = split3(jnp.concatenate(lses[n], axis=0))
            fetched[block] = scores[block] = weights[block] = products[block] = None


def merge_kernel(keep, *refs):
    ins, out_ref = refs[:-1], refs[-1]
    lses = [join3(r[ROWS:, :]) for r in ins]
    top = functools.reduce(jnp.maximum, lses)
    parts = [jnp.exp2(s - top) for s in lses]
    total = functools.reduce(jnp.add, parts)
    parts = [p / total for p in parts]
    for b in range(SEGB):
        rows = slice(b * BS, (b + 1) * BS)
        acc = jnp.zeros((BS, HD), F32)
        for r, p in zip(ins, parts):
            acc = acc + jnp.transpose(jnp.broadcast_to(p[b : b + 1, :], (BS, HD))) * r[rows, :].astype(F32)
        out_ref[rows, :] = acc.astype(out_ref.dtype)
    if keep:
        out_ref[ROWS:, :] = split3(top + jnp.log2(total))


def unpack_kernel(in_ref, out_ref):
    for h in range(HEADS):
        out_ref[:, h * HD : (h + 1) * HD] = in_ref[h]


def call(kernel, outs, specs, *args, scratch=(), flops=0, moved=1 << 18, vmem=24):
    return pl.pallas_call(
        kernel,
        out_shape=outs,
        in_specs=specs,
        out_specs=jax.tree.map(lambda _: VMEM, outs),
        scratch_shapes=list(scratch),
        compiler_params=pltpu.CompilerParams(vmem_limit_bytes=vmem << 20),
        cost_estimate=pl.CostEstimate(flops=flops, bytes_accessed=moved, transcendentals=0),
    )(*args)


def attend(queries, kvs, old=None):
    n = len(queries)
    if old is None:
        outs = [jax.ShapeDtypeStruct((2, ROWS, HD), F32)] * n
        unit = 4
    else:
        outs = [jax.ShapeDtypeStruct((ROWS + LSE, HD), BF)] * n
        unit = 8
    ins = [*queries, *kvs, *(old or [])]
    return call(
        functools.partial(attend_kernel, n, unit, old is None),
        outs, [VMEM] * len(ins), *ins,
        scratch=[pltpu.VMEM((n * SEGB, HD), jnp.int32), pltpu.SMEM((n * SEGB, HD), jnp.int32), pltpu.SemaphoreType.DMA],
        flops=n * (3 if old is None else 1) * (1 << 27), moved=2 << 20,
    )


def merge(keep, flops, *ins):
    out = jax.ShapeDtypeStruct((ROWS + LSE if keep else ROWS, HD), BF)
    return call(functools.partial(merge_kernel, keep), out, [VMEM] * len(ins), *ins, flops=flops)


def shards(queries, keys, values, block_mask):
    packed, picks = call(
        pack_kernel,
        (jax.ShapeDtypeStruct((NU, 3 * TOK, HD), BF), jax.ShapeDtypeStruct((PICKS, HD), BF)),
        [HBM] * 4, queries, keys, values, block_mask,
        scratch=[pltpu.VMEM(queries.shape, BF)] * 3
        + [pltpu.VMEM(block_mask.shape[1:], jnp.int32), pltpu.SemaphoreType.DMA((4,))],
        vmem=60,
    )
    got = exchange(packed, ("y", "zl"))
    k0 = got[:, TOK:]
    q0 = jnp.concatenate([got[:, :TOK].reshape(ROWS, HD), picks], axis=0)

    own = jnp.stack([k0, shift(k0, "core", 1)])
    near = ring_step(own)
    q1, q2, q3 = (shift(q0, "x", dx) for dx in (1, 2, 3))
    near, q1, q2, q3 = lax.optimization_barrier((near, q1, q2, q3))
    half = lax.dynamic_slice_in_dim(near, lax.axis_index("core") * (NU // 2), NU // 2, axis=1)
    last = ring_step(half)
    far = shift(near, "core", 1)
    old = attend([q0, q1, q2, q3], [own, near, far])

    last, *old = lax.optimization_barrier((last, *old))
    kvs = [jnp.concatenate([last, shift(last, "core", 1)], axis=0)]
    (o2,) = attend([q2], kvs, [old[2]])
    o2, *kvs = lax.optimization_barrier((o2, *kvs))
    back2 = shift(o2, "x", -2)
    o1, o3 = attend([q1, q3], kvs, [old[1], old[3]])
    o1, o3, *kvs = lax.optimization_barrier((o1, o3, *kvs))
    back1, back3 = shift(o1, "x", -1), shift(o3, "x", -3)
    (o0,) = attend([q0], kvs, [old[0]])
    first = merge(True, 1 << 33, o0, back2)
    whole = merge(False, 0, first, back1, back3)
    home = exchange(whole.reshape(NU, TOK, HD), ("y", "zl"))
    return call(unpack_kernel, jax.ShapeDtypeStruct((TOK, HEADS * HD), BF), [VMEM], home)


def solution(mesh):
    fine = Mesh(mesh.devices.reshape(NX, NZ, NC, NU // 2, 2), AXES)
    tokens = P(AXES, None)
    placed = (tokens, tokens, tokens, P(None, AXES[:3], None))
    return jax.shard_map(shards, mesh=fine, in_specs=placed, out_specs=tokens, check_vma=False)
```

```python
import functools
import math

import jax
import jax.numpy as jnp
from jax import lax
from jax.experimental import pallas as pl
from jax.experimental.pallas import tpu as pltpu
from jax.sharding import Mesh, PartitionSpec as P

BF = jnp.bfloat16
F32 = jnp.float32
NX, NZ, NC, NU = 4, 4, 2, 16
HEADS, HD, BS, TOK = 12, 128, 128, 64
SEGB = 8
ROWS = SEGB * BS
PICKS = 16
LSE = 32
STEPS = 4
EXP2 = math.log2(math.e) / math.sqrt(HD)
AXES = ("x", "zh", "core", "y", "zl")
VMEM = pl.BlockSpec(memory_space=pltpu.VMEM)
HBM = pl.BlockSpec(memory_space=pltpu.HBM)


def shift(field, axis, by):
    n = lax.axis_size(axis)
    return lax.ppermute(field, axis, [(i, (i + by) % n) for i in range(n)])


def ring_step(field):
    pairs = [(z * NC + c, (z + (1, -1)[c]) % NZ * NC + c) for z in range(NZ) for c in range(NC)]
    return lax.ppermute(field, ("zh", "core"), pairs)


def half(field):
    return lax.dynamic_slice_in_dim(field, lax.axis_index("core") * (NU // 2), NU // 2, axis=0)


def exchange(field, axes):
    return lax.all_to_all(field, axes, split_axis=0, concat_axis=0, tiled=True)


def pack_kernel(q_hbm, k_hbm, v_hbm, mask_hbm, out_ref, picks_ref, q_ref, k_ref, v_ref, mask_ref, sems):
    head = jnp.minimum(lax.axis_index("y") * 2 + lax.axis_index("zl"), HEADS - 1)
    pairs = ((q_hbm, q_ref), (k_hbm, k_ref), (v_hbm, v_ref), (mask_hbm.at[head], mask_ref))
    copies = [pltpu.make_async_copy(src, dst, sems.at[i]) for i, (src, dst) in enumerate(pairs)]
    for copy in copies:
        copy.start()
    for s in range(HEADS, NU):
        out_ref[s] = jnp.zeros((3 * TOK, HD), BF)
    for n, ref in enumerate((q_ref, k_ref, v_ref)):
        copies[n].wait()
        for h in range(HEADS):
            out_ref[h, n * TOK : (n + 1) * TOK, :] = ref[:, h * HD : (h + 1) * HD]
    copies[3].wait()
    live = mask_ref[...].astype(F32).astype(BF)
    cols = live.shape[1]
    i = lax.broadcasted_iota(jnp.int32, (cols, HD), 0)
    g = lax.broadcasted_iota(jnp.int32, (cols, HD), 1)
    weight = jnp.where(i // SEGB == g, i % SEGB, 0).astype(F32).astype(BF)
    picks = jnp.dot(live, weight, preferred_element_type=F32)
    picks_ref[...] = jnp.concatenate([picks, jnp.zeros((PICKS - SEGB, HD), F32)], axis=0).astype(BF)


def split3(lse):
    hi = lse.astype(BF).astype(F32)
    mid = (lse - hi).astype(BF).astype(F32)
    return jnp.concatenate([hi, mid, lse - hi - mid, jnp.zeros_like(hi)], axis=0).astype(BF)


def join3(rows):
    rows = rows.astype(F32)
    return rows[0:SEGB] + rows[SEGB : 2 * SEGB] + rows[2 * SEGB : 3 * SEGB]


def attend_kernel(chunks, unit, opening, *refs):
    n_kv = 3 if opening else 1
    q_refs, kv_refs, rest = refs[:chunks], refs[chunks : chunks + n_kv], refs[chunks + n_kv :]
    old_refs = () if opening else rest[:chunks]
    rest = rest[len(old_refs) :]
    out_refs, (flat_ref, picks_ref, sem) = rest[:chunks], rest[chunks:]
    for n, q_ref in enumerate(q_refs):
        flat_ref[n * SEGB : (n + 1) * SEGB, :] = q_ref[ROWS:, :].astype(F32)[:SEGB].astype(jnp.int32)
    fetch = pltpu.make_async_copy(flat_ref, picks_ref, sem)
    fetch.start()
    x, z, c = lax.axis_index("x"), lax.axis_index("zh"), lax.axis_index("core")
    if opening:
        own, near, far = kv_refs
        before, after = z + NZ - 1 + 2 * c, z + NZ + 1 - 2 * c
        groups = [(own, 0, z, c), (own, 1, z, 1 - c), (near, 0, before, c), (near, 1, before, 1 - c)]
        groups += [(far, 0, after, 1 - c), (far, 1, after, c)]
    else:
        groups = [(kv_refs[0], 0, z + 2, c), (kv_refs[0], 1, z + 2, 1 - c)]
    columns = [(x * NZ + lax.rem(zz, NZ)) * NC + cc for _, _, zz, cc in groups]
    pairs = len(groups) // 2

    def pick(group, j):
        ref, n = group[:2]
        if opening:
            return ref[n, pl.ds(2 * j, 2)]
        return ref[jnp.where(j // (SEGB // 2) == c, n, 3 - n), pl.ds(2 * lax.rem(j, SEGB // 2), 2)]

    fetch.wait()
    blocks = [(n, b) for n in range(chunks) for b in range(SEGB)]
    units = [blocks[i : i + unit] for i in range(0, len(blocks), unit)]
    fetched, scores, weights, peaks, totals, products = {}, {}, {}, {}, {}, {}
    lses = [[] for _ in q_refs]
    for t in range(len(units) + 2):
        ahead, here, last = (units[i] if 0 <= i < len(units) else [] for i in (t, t - 1, t - 2))
        for n, b in ahead:
            keys, values = [], []
            for group, column in zip(groups, columns):
                both = pick(group, picks_ref[n * SEGB + b, column])
                keys.append(both[:, :TOK, :].reshape(BS, HD))
                values.append(both[:, TOK:, :].reshape(BS, HD))
            fetched[n, b] = q_refs[n][b * BS : (b + 1) * BS, :], keys, values
            scores[n, b] = []
        for block in here:
            weights[block], peaks[block], totals[block] = [], [], []
        for block in last:
            products[block] = []
        for step in range(STEPS):
            pair = slice(2 * step, 2 * step + 2)
            rows = slice(step * BS // STEPS, (step + 1) * BS // STEPS)
            for i in range(unit):
                if i < len(ahead) and step < pairs:
                    q, keys, _ = fetched[ahead[i]]
                    both = jnp.concatenate(keys[pair], axis=0)
                    scores[ahead[i]].append(
                        lax.dot_general(q, both, (((1,), (1,)), ((), ())), preferred_element_type=F32)
                    )
                if i < len(here):
                    part = [s[rows] for s in scores[here[i]]]
                    peak = jnp.max(functools.reduce(jnp.maximum, part), axis=1, keepdims=True)
                    w = [jnp.exp2((s - peak) * EXP2) for s in part]
                    totals[here[i]].append(jnp.sum(functools.reduce(jnp.add, w), axis=1, keepdims=True))
                    peaks[here[i]].append(peak)
                    weights[here[i]].append([p.astype(BF) for p in w])
                if i < len(last) and step < pairs:
                    w = jnp.concatenate([p[step] for p in weights[last[i]]], axis=0)
                    both = jnp.concatenate(fetched[last[i]][2][pair], axis=0)
                    products[last[i]].append(jnp.dot(w, both, preferred_element_type=F32))
        for block in last:
            n, b = block
            peak, total = jnp.concatenate(peaks[block], axis=0), jnp.concatenate(totals[block], axis=0)
            rows = slice(b * BS, (b + 1) * BS)
            o = functools.reduce(jnp.add, products[block]) * (1.0 / total)
            lse = jnp.broadcast_to(peak * EXP2 + jnp.log2(total), (BS, HD))
            if opening:
                out_refs[n][0, rows, :] = o
                out_refs[n][1, rows, :] = lse
            else:
                old, old_lse = old_refs[n][0, rows, :], old_refs[n][1, rows, :]
                top = jnp.maximum(lse, old_lse)
                share, old_share = jnp.exp2(lse - top), jnp.exp2(old_lse - top)
                total = share + old_share
                out_refs[n][rows, :] = ((o * share + old * old_share) * (1.0 / total)).astype(BF)
                lses[n].append(jnp.transpose(top + jnp.log2(total))[0:1, :])
                if b == SEGB - 1:
                    out_refs[n][ROWS:, :] = split3(jnp.concatenate(lses[n], axis=0))
            fetched[block] = scores[block] = weights[block] = products[block] = None


def merge_kernel(keep, *refs):
    ins, out_ref = refs[:-1], refs[-1]
    lses = [join3(r[ROWS:, :]) for r in ins]
    top = functools.reduce(jnp.maximum, lses)
    parts = [jnp.exp2(s - top) for s in lses]
    total = functools.reduce(jnp.add, parts)
    parts = [p / total for p in parts]
    for b in range(SEGB):
        rows = slice(b * BS, (b + 1) * BS)
        acc = jnp.zeros((BS, HD), F32)
        for r, p in zip(ins, parts):
            acc = acc + jnp.transpose(jnp.broadcast_to(p[b : b + 1, :], (BS, HD))) * r[rows, :].astype(F32)
        out_ref[rows, :] = acc.astype(out_ref.dtype)
    if keep:
        out_ref[ROWS:, :] = split3(top + jnp.log2(total))


def unpack_kernel(in_ref, out_ref):
    for h in range(HEADS):
        out_ref[:, h * HD : (h + 1) * HD] = in_ref[h]


def call(kernel, outs, specs, *args, scratch=(), flops=0, moved=1 << 18, vmem=24):
    return pl.pallas_call(
        kernel,
        out_shape=outs,
        in_specs=specs,
        out_specs=jax.tree.map(lambda _: VMEM, outs),
        scratch_shapes=list(scratch),
        compiler_params=pltpu.CompilerParams(vmem_limit_bytes=vmem << 20),
        cost_estimate=pl.CostEstimate(flops=flops, bytes_accessed=moved, transcendentals=0),
    )(*args)


def attend(queries, kvs, old=None):
    n = len(queries)
    if old is None:
        outs = [jax.ShapeDtypeStruct((2, ROWS, HD), F32)] * n
        unit = 4
    else:
        outs = [jax.ShapeDtypeStruct((ROWS + LSE, HD), BF)] * n
        unit = 8
    ins = [*queries, *kvs, *(old or [])]
    return call(
        functools.partial(attend_kernel, n, unit, old is None),
        outs, [VMEM] * len(ins), *ins,
        scratch=[pltpu.VMEM((n * SEGB, HD), jnp.int32), pltpu.SMEM((n * SEGB, HD), jnp.int32), pltpu.SemaphoreType.DMA],
        flops=n * (3 if old is None else 1) * (1 << 27), moved=2 << 20,
    )


def merge(keep, flops, *ins):
    out = jax.ShapeDtypeStruct((ROWS + LSE if keep else ROWS, HD), BF)
    return call(functools.partial(merge_kernel, keep), out, [VMEM] * len(ins), *ins, flops=flops)


def shards(queries, keys, values, block_mask):
    packed, picks = call(
        pack_kernel,
        (jax.ShapeDtypeStruct((NU, 3 * TOK, HD), BF), jax.ShapeDtypeStruct((PICKS, HD), BF)),
        [HBM] * 4, queries, keys, values, block_mask,
        scratch=[pltpu.VMEM(queries.shape, BF)] * 3
        + [pltpu.VMEM(block_mask.shape[1:], jnp.int32), pltpu.SemaphoreType.DMA((4,))],
        vmem=60,
    )
    got = exchange(packed, ("y", "zl"))
    k0 = got[:, TOK:]
    q0 = jnp.concatenate([got[:, :TOK].reshape(ROWS, HD), picks], axis=0)

    near0 = ring_step(k0)
    other = shift(k0, "core", 1)
    near1 = ring_step(other)
    q1, q2, q3 = (shift(q0, "x", dx) for dx in (1, 2, 3))
    near0, q1, q2, q3 = lax.optimization_barrier((near0, q1, q2, q3))
    last0, last1 = ring_step(half(near0)), ring_step(half(near1))
    near0, near1, last0 = lax.optimization_barrier((near0, near1, last0))
    own, near = jnp.stack([k0, other]), jnp.stack([near0, near1])
    far = shift(near, "core", 1)
    old = attend([q0, q1, q2, q3], [own, near, far])

    last0, last1, *old = lax.optimization_barrier((last0, last1, *old))
    last = jnp.stack([last0, last1])
    kvs = [jnp.concatenate([last, shift(last, "core", 1)], axis=0)]
    (o2,) = attend([q2], kvs, [old[2]])
    o2, *kvs = lax.optimization_barrier((o2, *kvs))
    back2 = shift(o2, "x", -2)
    o1, o3 = attend([q1, q3], kvs, [old[1], old[3]])
    o1, o3, *kvs = lax.optimization_barrier((o1, o3, *kvs))
    back1, back3 = shift(o1, "x", -1), shift(o3, "x", -3)
    (o0,) = attend([q0], kvs, [old[0]])
    first = merge(True, 1 << 33, o0, back2)
    whole = merge(False, 0, first, back1, back3)
    home = exchange(whole.reshape(NU, TOK, HD), ("y", "zl"))
    return call(unpack_kernel, jax.ShapeDtypeStruct((TOK, HEADS * HD), BF), [VMEM], home)


def solution(mesh):
    fine = Mesh(mesh.devices.reshape(NX, NZ, NC, NU // 2, 2), AXES)
    tokens = P(AXES, None)
    placed = (tokens, tokens, tokens, P(None, AXES[:3], None))
    return jax.shard_map(shards, mesh=fine, in_specs=placed, out_specs=tokens, check_vma=False)
```

```python
import functools
import math

import jax
import jax.numpy as jnp
from jax import lax
from jax.experimental import pallas as pl
from jax.experimental.pallas import tpu as pltpu
from jax.sharding import Mesh, PartitionSpec as P

BF = jnp.bfloat16
F32 = jnp.float32
NX, NZ, NC, NU = 4, 4, 2, 16
HEADS, HD, BS, TOK = 12, 128, 128, 64
SEGB = 8
ROWS = SEGB * BS
PICKS = 16
LSE = 32
STEPS = 4
EXP2 = math.log2(math.e) / math.sqrt(HD)
AXES = ("x", "zh", "core", "y", "zl")
VMEM = pl.BlockSpec(memory_space=pltpu.VMEM)
HBM = pl.BlockSpec(memory_space=pltpu.HBM)


def shift(field, axis, by):
    n = lax.axis_size(axis)
    return lax.ppermute(field, axis, [(i, (i + by) % n) for i in range(n)])


def ring_step(field):
    pairs = [(z * NC + c, (z + (1, -1)[c]) % NZ * NC + c) for z in range(NZ) for c in range(NC)]
    return lax.ppermute(field, ("zh", "core"), pairs)


def exchange(field, axes):
    return lax.all_to_all(field, axes, split_axis=0, concat_axis=0, tiled=True)


def pack_kernel(q_hbm, k_hbm, v_hbm, mask_hbm, out_ref, picks_ref, q_ref, k_ref, v_ref, mask_ref, sems):
    head = jnp.minimum(lax.axis_index("y") * 2 + lax.axis_index("zl"), HEADS - 1)
    pairs = ((q_hbm, q_ref), (k_hbm, k_ref), (v_hbm, v_ref), (mask_hbm.at[head], mask_ref))
    copies = [pltpu.make_async_copy(src, dst, sems.at[i]) for i, (src, dst) in enumerate(pairs)]
    for copy in copies:
        copy.start()
    for s in range(HEADS, NU):
        out_ref[s] = jnp.zeros((3 * TOK, HD), BF)
    for n, ref in enumerate((q_ref, k_ref, v_ref)):
        copies[n].wait()
        for h in range(HEADS):
            out_ref[h, n * TOK : (n + 1) * TOK, :] = ref[:, h * HD : (h + 1) * HD]
    copies[3].wait()
    live = mask_ref[...].astype(F32).astype(BF)
    cols = live.shape[1]
    i = lax.broadcasted_iota(jnp.int32, (cols, HD), 0)
    g = lax.broadcasted_iota(jnp.int32, (cols, HD), 1)
    weight = jnp.where(i // SEGB == g, i % SEGB, 0).astype(F32).astype(BF)
    picks = jnp.dot(live, weight, preferred_element_type=F32)
    picks_ref[...] = jnp.concatenate([picks, jnp.zeros((PICKS - SEGB, HD), F32)], axis=0).astype(BF)


def split3(lse):
    hi = lse.astype(BF).astype(F32)
    mid = (lse - hi).astype(BF).astype(F32)
    return jnp.concatenate([hi, mid, lse - hi - mid, jnp.zeros_like(hi)], axis=0).astype(BF)


def join3(rows):
    rows = rows.astype(F32)
    return rows[0:SEGB] + rows[SEGB : 2 * SEGB] + rows[2 * SEGB : 3 * SEGB]


def attend_kernel(chunks, unit, opening, *refs):
    n_kv = 2
    q_refs, kv_refs, rest = refs[:chunks], refs[chunks : chunks + n_kv], refs[chunks + n_kv :]
    old_refs = () if opening else rest[:chunks]
    rest = rest[len(old_refs) :]
    out_refs, (flat_ref, picks_ref, sem) = rest[:chunks], rest[chunks:]
    for n, q_ref in enumerate(q_refs):
        flat_ref[n * SEGB : (n + 1) * SEGB, :] = q_ref[ROWS:, :].astype(F32)[:SEGB].astype(jnp.int32)
    fetch = pltpu.make_async_copy(flat_ref, picks_ref, sem)
    fetch.start()
    x, z, c = lax.axis_index("x"), lax.axis_index("zh"), lax.axis_index("core")
    before, after = z + NZ - 1 + 2 * c, z + NZ + 1 - 2 * c
    first, second = kv_refs
    if opening:
        groups = [(first, 0, z, c), (first, 1, z, 1 - c), (second, 0, before, c), (second, 1, before, 1 - c)]
    else:
        groups = [(first, 0, after, 1 - c), (first, 1, after, c), (second, 0, z + 2, c), (second, 1, z + 2, 1 - c)]
    columns = [(x * NZ + lax.rem(zz, NZ)) * NC + cc for _, _, zz, cc in groups]
    pairs = len(groups) // 2

    def pick(group, j):
        ref, n = group[:2]
        if opening or ref is first:
            return ref[n, pl.ds(2 * j, 2)]
        return ref[jnp.where(j // (SEGB // 2) == c, n, 3 - n), pl.ds(2 * lax.rem(j, SEGB // 2), 2)]

    fetch.wait()
    blocks = [(n, b) for n in range(chunks) for b in range(SEGB)]
    units = [blocks[i : i + unit] for i in range(0, len(blocks), unit)]
    fetched, scores, weights, peaks, totals, products = {}, {}, {}, {}, {}, {}
    lses = [[] for _ in q_refs]
    for t in range(len(units) + 2):
        ahead, here, last = (units[i] if 0 <= i < len(units) else [] for i in (t, t - 1, t - 2))
        for n, b in ahead:
            keys, values = [], []
            for group, column in zip(groups, columns):
                both = pick(group, picks_ref[n * SEGB + b, column])
                keys.append(both[:, :TOK, :].reshape(BS, HD))
                values.append(both[:, TOK:, :].reshape(BS, HD))
            fetched[n, b] = q_refs[n][b * BS : (b + 1) * BS, :], keys, values
            scores[n, b] = []
        for block in here:
            weights[block], peaks[block], totals[block] = [], [], []
        for block in last:
            products[block] = []
        for step in range(STEPS):
            pair = slice(2 * step, 2 * step + 2)
            rows = slice(step * BS // STEPS, (step + 1) * BS // STEPS)
            for i in range(unit):
                if i < len(ahead) and step < pairs:
                    q, keys, _ = fetched[ahead[i]]
                    both = jnp.concatenate(keys[pair], axis=0)
                    scores[ahead[i]].append(
                        lax.dot_general(q, both, (((1,), (1,)), ((), ())), preferred_element_type=F32)
                    )
                if i < len(here):
                    part = [s[rows] for s in scores[here[i]]]
                    peak = jnp.max(functools.reduce(jnp.maximum, part), axis=1, keepdims=True)
                    w = [jnp.exp2((s - peak) * EXP2) for s in part]
                    totals[here[i]].append(jnp.sum(functools.reduce(jnp.add, w), axis=1, keepdims=True))
                    peaks[here[i]].append(peak)
                    weights[here[i]].append([p.astype(BF) for p in w])
                if i < len(last) and step < pairs:
                    w = jnp.concatenate([p[step] for p in weights[last[i]]], axis=0)
                    both = jnp.concatenate(fetched[last[i]][2][pair], axis=0)
                    products[last[i]].append(jnp.dot(w, both, preferred_element_type=F32))
        for block in last:
            n, b = block
            peak, total = jnp.concatenate(peaks[block], axis=0), jnp.concatenate(totals[block], axis=0)
            rows = slice(b * BS, (b + 1) * BS)
            o = functools.reduce(jnp.add, products[block]) * (1.0 / total)
            lse = jnp.broadcast_to(peak * EXP2 + jnp.log2(total), (BS, HD))
            if opening:
                out_refs[n][0, rows, :] = o
                out_refs[n][1, rows, :] = lse
            else:
                old, old_lse = old_refs[n][0, rows, :], old_refs[n][1, rows, :]
                top = jnp.maximum(lse, old_lse)
                share, old_share = jnp.exp2(lse - top), jnp.exp2(old_lse - top)
                total = share + old_share
                out_refs[n][rows, :] = ((o * share + old * old_share) * (1.0 / total)).astype(BF)
                lses[n].append(jnp.transpose(top + jnp.log2(total))[0:1, :])
                if b == SEGB - 1:
                    out_refs[n][ROWS:, :] = split3(jnp.concatenate(lses[n], axis=0))
            fetched[block] = scores[block] = weights[block] = products[block] = None


def merge_kernel(keep, *refs):
    ins, out_ref = refs[:-1], refs[-1]
    lses = [join3(r[ROWS:, :]) for r in ins]
    top = functools.reduce(jnp.maximum, lses)
    parts = [jnp.exp2(s - top) for s in lses]
    total = functools.reduce(jnp.add, parts)
    parts = [p / total for p in parts]
    for b in range(SEGB):
        rows = slice(b * BS, (b + 1) * BS)
        acc = jnp.zeros((BS, HD), F32)
        for r, p in zip(ins, parts):
            acc = acc + jnp.transpose(jnp.broadcast_to(p[b : b + 1, :], (BS, HD))) * r[rows, :].astype(F32)
        out_ref[rows, :] = acc.astype(out_ref.dtype)
    if keep:
        out_ref[ROWS:, :] = split3(top + jnp.log2(total))


def unpack_kernel(in_ref, out_ref):
    for h in range(HEADS):
        out_ref[:, h * HD : (h + 1) * HD] = in_ref[h]


def call(kernel, outs, specs, *args, scratch=(), flops=0, moved=1 << 18, vmem=24):
    return pl.pallas_call(
        kernel,
        out_shape=outs,
        in_specs=specs,
        out_specs=jax.tree.map(lambda _: VMEM, outs),
        scratch_shapes=list(scratch),
        compiler_params=pltpu.CompilerParams(vmem_limit_bytes=vmem << 20),
        cost_estimate=pl.CostEstimate(flops=flops, bytes_accessed=moved, transcendentals=0),
    )(*args)


def attend(queries, kvs, old=None):
    n = len(queries)
    if old is None:
        outs = [jax.ShapeDtypeStruct((2, ROWS, HD), F32)] * n
        unit = 4
    else:
        outs = [jax.ShapeDtypeStruct((ROWS + LSE, HD), BF)] * n
        unit = 8
    ins = [*queries, *kvs, *(old or [])]
    return call(
        functools.partial(attend_kernel, n, unit, old is None),
        outs, [VMEM] * len(ins), *ins,
        scratch=[pltpu.VMEM((n * SEGB, HD), jnp.int32), pltpu.SMEM((n * SEGB, HD), jnp.int32), pltpu.SemaphoreType.DMA],
        flops=n * (1 << 28), moved=2 << 20,
    )


def merge(keep, flops, *ins):
    out = jax.ShapeDtypeStruct((ROWS + LSE if keep else ROWS, HD), BF)
    return call(functools.partial(merge_kernel, keep), out, [VMEM] * len(ins), *ins, flops=flops)


def shards(queries, keys, values, block_mask):
    packed, picks = call(
        pack_kernel,
        (jax.ShapeDtypeStruct((NU, 3 * TOK, HD), BF), jax.ShapeDtypeStruct((PICKS, HD), BF)),
        [HBM] * 4, queries, keys, values, block_mask,
        scratch=[pltpu.VMEM(queries.shape, BF)] * 3
        + [pltpu.VMEM(block_mask.shape[1:], jnp.int32), pltpu.SemaphoreType.DMA((4,))],
        vmem=60,
    )
    got = exchange(packed, ("y", "zl"))
    k0 = got[:, TOK:]
    q0 = jnp.concatenate([got[:, :TOK].reshape(ROWS, HD), picks], axis=0)

    own = jnp.stack([k0, shift(k0, "core", 1)])
    near = ring_step(own)
    q1, q2, q3 = (shift(q0, "x", dx) for dx in (1, 2, 3))
    near, q1, q2, q3 = lax.optimization_barrier((near, q1, q2, q3))
    half = lax.dynamic_slice_in_dim(near, lax.axis_index("core") * (NU // 2), NU // 2, axis=1)
    last = ring_step(half)
    old = attend([q0, q1, q2, q3], [own, near])

    near, last, *old = lax.optimization_barrier((near, last, *old))
    far = shift(jnp.concatenate([near, last], axis=1), "core", 1)
    kvs = [far, jnp.concatenate([last, far[:, NU:]], axis=0)]
    (o2,) = attend([q2], kvs, [old[2]])
    o2, *kvs = lax.optimization_barrier((o2, *kvs))
    back2 = shift(o2, "x", -2)
    o1, o3 = attend([q1, q3], kvs, [old[1], old[3]])
    o1, o3, *kvs = lax.optimization_barrier((o1, o3, *kvs))
    back1, back3 = shift(o1, "x", -1), shift(o3, "x", -3)
    (o0,) = attend([q0], kvs, [old[0]])
    first = merge(True, 1 << 33, o0, back2)
    whole = merge(False, 0, first, back1, back3)
    home = exchange(whole.reshape(NU, TOK, HD), ("y", "zl"))
    return call(unpack_kernel, jax.ShapeDtypeStruct((TOK, HEADS * HD), BF), [VMEM], home)


def solution(mesh):
    fine = Mesh(mesh.devices.reshape(NX, NZ, NC, NU // 2, 2), AXES)
    tokens = P(AXES, None)
    placed = (tokens, tokens, tokens, P(None, AXES[:3], None))
    return jax.shard_map(shards, mesh=fine, in_specs=placed, out_specs=tokens, check_vma=False)
```

```python
import functools
import math

import jax
import jax.numpy as jnp
from jax import lax
from jax.experimental import pallas as pl
from jax.experimental.pallas import tpu as pltpu
from jax.sharding import Mesh, PartitionSpec as P

BF = jnp.bfloat16
F32 = jnp.float32
NX, NZ, NC, NU = 4, 4, 2, 16
HEADS, HD, BS, TOK = 12, 128, 128, 64
SEGB = 8
ROWS = SEGB * BS
PICKS = 16
LSE = 32
STEPS = 4
EXP2 = math.log2(math.e) / math.sqrt(HD)
AXES = ("x", "zh", "core", "y", "zl")
VMEM = pl.BlockSpec(memory_space=pltpu.VMEM)
HBM = pl.BlockSpec(memory_space=pltpu.HBM)


def shift(field, axis, by):
    n = lax.axis_size(axis)
    return lax.ppermute(field, axis, [(i, (i + by) % n) for i in range(n)])


def ring_step(field):
    pairs = [(z * NC + c, (z + (1, -1)[c]) % NZ * NC + c) for z in range(NZ) for c in range(NC)]
    return lax.ppermute(field, ("zh", "core"), pairs)


def exchange(field, axes):
    return lax.all_to_all(field, axes, split_axis=0, concat_axis=0, tiled=True)


def pack_kernel(q_hbm, k_hbm, v_hbm, mask_hbm, out_ref, picks_ref, q_ref, k_ref, v_ref, mask_ref, sems):
    head = jnp.minimum(lax.axis_index("y") * 2 + lax.axis_index("zl"), HEADS - 1)
    pairs = ((q_hbm, q_ref), (k_hbm, k_ref), (v_hbm, v_ref), (mask_hbm.at[head], mask_ref))
    copies = [pltpu.make_async_copy(src, dst, sems.at[i]) for i, (src, dst) in enumerate(pairs)]
    for copy in copies:
        copy.start()
    for s in range(HEADS, NU):
        out_ref[s] = jnp.zeros((3 * TOK, HD), BF)
    for n, ref in enumerate((q_ref, k_ref, v_ref)):
        copies[n].wait()
        for h in range(HEADS):
            out_ref[h, n * TOK : (n + 1) * TOK, :] = ref[:, h * HD : (h + 1) * HD]
    copies[3].wait()
    live = mask_ref[...].astype(F32).astype(BF)
    cols = live.shape[1]
    i = lax.broadcasted_iota(jnp.int32, (cols, HD), 0)
    g = lax.broadcasted_iota(jnp.int32, (cols, HD), 1)
    weight = jnp.where(i // SEGB == g, i % SEGB, 0).astype(F32).astype(BF)
    picks = jnp.dot(live, weight, preferred_element_type=F32)
    picks_ref[...] = jnp.concatenate([picks, jnp.zeros((PICKS - SEGB, HD), F32)], axis=0).astype(BF)


def split3(lse):
    hi = lse.astype(BF).astype(F32)
    mid = (lse - hi).astype(BF).astype(F32)
    return jnp.concatenate([hi, mid, lse - hi - mid, jnp.zeros_like(hi)], axis=0).astype(BF)


def join3(rows):
    rows = rows.astype(F32)
    return rows[0:SEGB] + rows[SEGB : 2 * SEGB] + rows[2 * SEGB : 3 * SEGB]


def attend_kernel(chunks, unit, opening, *refs):
    n_kv = 3 if opening else 1
    q_refs, kv_refs, rest = refs[:chunks], refs[chunks : chunks + n_kv], refs[chunks + n_kv :]
    old_refs = () if opening else rest[:chunks]
    rest = rest[len(old_refs) :]
    out_refs, (flat_ref, picks_ref, sem) = rest[:chunks], rest[chunks:]
    for n, q_ref in enumerate(q_refs):
        flat_ref[n * SEGB : (n + 1) * SEGB, :] = q_ref[ROWS:, :].astype(F32)[:SEGB].astype(jnp.int32)
    fetch = pltpu.make_async_copy(flat_ref, picks_ref, sem)
    fetch.start()
    x, z, c = lax.axis_index("x"), lax.axis_index("zh"), lax.axis_index("core")
    if opening:
        own, near, far = kv_refs
        before, after = z + NZ - 1 + 2 * c, z + NZ + 1 - 2 * c
        groups = [(own, 0, z, c), (own, 1, z, 1 - c), (near, 0, before, c), (near, 1, before, 1 - c)]
        groups += [(far, 0, after, 1 - c), (far, 1, after, c)]
    else:
        groups = [(kv_refs[0], 0, z + 2, c), (kv_refs[0], 1, z + 2, 1 - c)]
    columns = [(x * NZ + lax.rem(zz, NZ)) * NC + cc for _, _, zz, cc in groups]
    pairs = len(groups) // 2

    def pick(group, j):
        ref, n = group[:2]
        if opening:
            return ref[n, pl.ds(2 * j, 2)]
        return ref[jnp.where(j // (SEGB // 2) == c, n, 3 - n), pl.ds(2 * lax.rem(j, SEGB // 2), 2)]

    fetch.wait()
    blocks = [(n, b) for n in range(chunks) for b in range(SEGB)]
    units = [blocks[i : i + unit] for i in range(0, len(blocks), unit)]
    fetched, scores, weights, peaks, totals, products = {}, {}, {}, {}, {}, {}
    lses = [[] for _ in q_refs]
    for t in range(len(units) + 2):
        ahead, here, last = (units[i] if 0 <= i < len(units) else [] for i in (t, t - 1, t - 2))
        for n, b in ahead:
            keys, values = [], []
            for group, column in zip(groups, columns):
                both = pick(group, picks_ref[n * SEGB + b, column])
                keys.append(both[:, :TOK, :].reshape(BS, HD))
                values.append(both[:, TOK:, :].reshape(BS, HD))
            fetched[n, b] = q_refs[n][b * BS : (b + 1) * BS, :], keys, values
            scores[n, b] = []
        for block in here:
            weights[block], peaks[block], totals[block] = [], [], []
        for block in last:
            products[block] = []
        for step in range(STEPS):
            pair = slice(2 * step, 2 * step + 2)
            rows = slice(step * BS // STEPS, (step + 1) * BS // STEPS)
            for i in range(unit):
                if i < len(ahead) and step < pairs:
                    q, keys, _ = fetched[ahead[i]]
                    both = jnp.concatenate(keys[pair], axis=0)
                    scores[ahead[i]].append(
                        lax.dot_general(q, both, (((1,), (1,)), ((), ())), preferred_element_type=F32)
                    )
                if i < len(here):
                    part = [s[rows] for s in scores[here[i]]]
                    peak = jnp.max(functools.reduce(jnp.maximum, part), axis=1, keepdims=True)
                    w = [jnp.exp2((s - peak) * EXP2) for s in part]
                    totals[here[i]].append(jnp.sum(functools.reduce(jnp.add, w), axis=1, keepdims=True))
                    peaks[here[i]].append(peak)
                    weights[here[i]].append([p.astype(BF) for p in w])
                if i < len(last) and step < pairs:
                    w = jnp.concatenate([p[step] for p in weights[last[i]]], axis=0)
                    both = jnp.concatenate(fetched[last[i]][2][pair], axis=0)
                    products[last[i]].append(jnp.dot(w, both, preferred_element_type=F32))
        for block in last:
            n, b = block
            peak, total = jnp.concatenate(peaks[block], axis=0), jnp.concatenate(totals[block], axis=0)
            rows = slice(b * BS, (b + 1) * BS)
            o = functools.reduce(jnp.add, products[block]) * (1.0 / total)
            lse = jnp.broadcast_to(peak * EXP2 + jnp.log2(total), (BS, HD))
            if opening:
                out_refs[n][0, rows, :] = o
                out_refs[n][1, rows, :] = lse
            else:
                old, old_lse = old_refs[n][0, rows, :], old_refs[n][1, rows, :]
                top = jnp.maximum(lse, old_lse)
                share, old_share = jnp.exp2(lse - top), jnp.exp2(old_lse - top)
                total = share + old_share
                out_refs[n][rows, :] = ((o * share + old * old_share) * (1.0 / total)).astype(BF)
                lses[n].append(jnp.transpose(top + jnp.log2(total))[0:1, :])
                if b == SEGB - 1:
                    out_refs[n][ROWS:, :] = split3(jnp.concatenate(lses[n], axis=0))
            fetched[block] = scores[block] = weights[block] = products[block] = None


def merge_kernel(keep, *refs):
    ins, out_ref = refs[:-1], refs[-1]
    lses = [join3(r[ROWS:, :]) for r in ins]
    top = functools.reduce(jnp.maximum, lses)
    parts = [jnp.exp2(s - top) for s in lses]
    total = functools.reduce(jnp.add, parts)
    parts = [p / total for p in parts]
    for b in range(SEGB):
        rows = slice(b * BS, (b + 1) * BS)
        acc = jnp.zeros((BS, HD), F32)
        for r, p in zip(ins, parts):
            acc = acc + jnp.transpose(jnp.broadcast_to(p[b : b + 1, :], (BS, HD))) * r[rows, :].astype(F32)
        out_ref[rows, :] = acc.astype(out_ref.dtype)
    if keep:
        out_ref[ROWS:, :] = split3(top + jnp.log2(total))


def unpack_kernel(in_ref, out_ref):
    for h in range(HEADS):
        out_ref[:, h * HD : (h + 1) * HD] = in_ref[h]


def call(kernel, outs, specs, *args, scratch=(), flops=0, moved=1 << 18, vmem=14):
    return pl.pallas_call(
        kernel,
        out_shape=outs,
        in_specs=specs,
        out_specs=jax.tree.map(lambda _: VMEM, outs),
        scratch_shapes=list(scratch),
        compiler_params=pltpu.CompilerParams(vmem_limit_bytes=vmem << 20),
        cost_estimate=pl.CostEstimate(flops=flops, bytes_accessed=moved, transcendentals=0),
    )(*args)


def attend(queries, kvs, old=None):
    n = len(queries)
    if old is None:
        outs = [jax.ShapeDtypeStruct((2, ROWS, HD), F32)] * n
        unit = 4
    else:
        outs = [jax.ShapeDtypeStruct((ROWS + LSE, HD), BF)] * n
        unit = 8
    ins = [*queries, *kvs, *(old or [])]
    return call(
        functools.partial(attend_kernel, n, unit, old is None),
        outs, [VMEM] * len(ins), *ins,
        scratch=[pltpu.VMEM((n * SEGB, HD), jnp.int32), pltpu.SMEM((n * SEGB, HD), jnp.int32), pltpu.SemaphoreType.DMA],
        flops=n * (3 if old is None else 1) * (1 << 27), moved=2 << 20,
    )


def merge(keep, flops, *ins):
    out = jax.ShapeDtypeStruct((ROWS + LSE if keep else ROWS, HD), BF)
    return call(functools.partial(merge_kernel, keep), out, [VMEM] * len(ins), *ins, flops=flops)


def shards(queries, keys, values, block_mask):
    packed, picks = call(
        pack_kernel,
        (jax.ShapeDtypeStruct((NU, 3 * TOK, HD), BF), jax.ShapeDtypeStruct((PICKS, HD), BF)),
        [HBM] * 4, queries, keys, values, block_mask,
        scratch=[pltpu.VMEM(queries.shape, BF)] * 3
        + [pltpu.VMEM(block_mask.shape[1:], jnp.int32), pltpu.SemaphoreType.DMA((4,))],
        vmem=60,
    )
    got = exchange(packed, ("y", "zl"))
    k0 = got[:, TOK:]
    q0 = jnp.concatenate([got[:, :TOK].reshape(ROWS, HD), picks], axis=0)

    own = jnp.stack([k0, shift(k0, "core", 1)])
    near = ring_step(own)
    q1, q2, q3 = (shift(q0, "x", dx) for dx in (1, 2, 3))
    near, q1, q2, q3 = lax.optimization_barrier((near, q1, q2, q3))
    half = lax.dynamic_slice_in_dim(near, lax.axis_index("core") * (NU // 2), NU // 2, axis=1)
    last = ring_step(half)
    far = shift(near, "core", 1)
    old = attend([q0, q1, q2, q3], [own, near, far])

    last, *old = lax.optimization_barrier((last, *old))
    kvs = [jnp.concatenate([last, shift(last, "core", 1)], axis=0)]
    (o2,) = attend([q2], kvs, [old[2]])
    o2, *kvs = lax.optimization_barrier((o2, *kvs))
    back2 = shift(o2, "x", -2)
    o1, o3 = attend([q1, q3], kvs, [old[1], old[3]])
    o1, o3, *kvs = lax.optimization_barrier((o1, o3, *kvs))
    back1, back3 = shift(o1, "x", -1), shift(o3, "x", -3)
    (o0,) = attend([q0], kvs, [old[0]])
    first = merge(True, 1 << 33, o0, back2)
    whole = merge(False, 0, first, back1, back3)
    home = exchange(whole.reshape(NU, TOK, HD), ("y", "zl"))
    return call(unpack_kernel, jax.ShapeDtypeStruct((TOK, HEADS * HD), BF), [VMEM], home)


def solution(mesh):
    fine = Mesh(mesh.devices.reshape(NX, NZ, NC, NU // 2, 2), AXES)
    tokens = P(AXES, None)
    placed = (tokens, tokens, tokens, P(None, AXES[:3], None))
    return jax.shard_map(shards, mesh=fine, in_specs=placed, out_specs=tokens, check_vma=False)
```
